512 devices in a mesh: tile: 64 (over z, y), mem: 8 (over x, core).
Axes of the slice: x: 4, y: 4, z: 16, core: 2. Of those that a mesh axis runs over, the one named last changes fastest.
Arguments:
- search_dir: float32 [5, 64, 128, 256], P(None, 'mem', 'tile'), may hold values from -6 to 6
- perturb: bfloat16 [5, 64, 128, 128, 256], P(None, None, 'mem', 'tile'), may hold values from -6 to 6
- smooth_y: float32 [128, 128], replicated, may hold values from -1 to 1
- smooth_x: float32 [256, 256], replicated, may hold values from -1 to 1
- vertical: float32 [64, 64], replicated, may hold values from -1 to 1
- level_scale: int32 [64], replicated, may hold values from 1 to 4
Outputs:
- increment: float32 [5, 64, 128, 256], P(None, 'mem', 'tile')
The draws below stay inside these ranges and needn't reach their ends.
All inputs are finite; a program needn't handle non-finite values.
Results may differ from the reference program's by a relative error of at most 0.0003.
Values sent between devices are 32-bit elements; how exact they have to be, the bound alone decides.
No kernel may reach another device: no remote copies, remote signals or barrier semaphores. Data moves between devices by JAX's collectives and lax.ppermute only.
A program may use at most 128 MiB of HBM per device.

```python
import jax
import jax.numpy as jnp
from jax import lax

NX = 256
NY = 128
LEVELS = 64
VARS = 5
PMAX = 4
MEMBERS = 128


def corr_matrix(key, size, span, reach, lower, upper):
    first, second = jax.random.split(key)
    rows = jnp.arange(size)[:, None]
    cols = jnp.arange(size)[None, :]
    distance = jnp.abs(rows - cols).astype(jnp.float32)
    diag_part = lower + (upper - lower) * jax.random.uniform(first, (size, size), jnp.float32)
    signs = jax.random.uniform(second, (size, size), jnp.float32, -1.0, 1.0)
    off_part = jnp.exp(-distance / span) * signs * (reach / jnp.sqrt(span))
    return jnp.where(rows == cols, diag_part, off_part)


def draw_smooth_y(key, part):
    key = jax.random.fold_in(key, 1)
    return corr_matrix(key, NY, NY / 16.0, 0.5, 0.87, 1.0)


def draw_smooth_x(key, part):
    key = jax.random.fold_in(key, 2)
    return corr_matrix(key, NX, NX / 16.0, 0.5, 0.87, 1.0)


def draw_vertical(key, part):
    key = jax.random.fold_in(key, 3)
    return corr_matrix(key, LEVELS, LEVELS / 16.0, 1.0, 0.8165, 0.9798)


def draw_level_scale(key, part):
    key = jax.random.fold_in(key, 4)
    first, second, third = jax.random.split(key, 3)
    values = jax.random.randint(first, (LEVELS,), 1, PMAX + 1)
    highest_at = jax.random.randint(second, (), 0, LEVELS)
    lowest_at = (highest_at + 1 + jax.random.randint(third, (), 0, LEVELS - 1)) % LEVELS
    values = values.at[highest_at].set(PMAX).at[lowest_at].set(1)
    return values.astype(jnp.int32)


def with_spikes(entries, stream_key, source, target, blocks, factor):
    def block_of(axis_at):
        return (jnp.arange(entries.shape[axis_at]) // (entries.shape[axis_at] // blocks)).reshape((-1,) + (1,) * (entries.ndim - 1 - axis_at))

    near = jax.random.permutation(stream_key, blocks)[block_of(target)]
    other_side = (block_of(target) + blocks // 2) % blocks
    return jnp.where((block_of(source) == near) | (block_of(source) == other_side), factor * entries, entries)


def block_scale(key, extent, cuts, low, high):
    def one(dim, parts):
        heights = jax.random.uniform(jax.random.fold_in(jax.random.fold_in(key, 6), dim), (parts,), jnp.float32, low / len(cuts), high / len(cuts))
        return jnp.repeat(jnp.exp(heights), extent[dim] // parts).reshape((-1,) + (1,) * (len(extent) - dim - 1))

    level = one(*cuts[0])
    for cut in cuts[1:]:
        level = level * one(*cut)
    return level


def gaussian(stream_key, shape, scale, bound, pieces=(), kind=jnp.bfloat16):
    loudness = block_scale(stream_key, shape, pieces, -0.22, 0.18) if pieces else 1.0
    entries = jax.random.normal(stream_key, shape, jnp.float32) * scale * loudness
    return jnp.minimum(jnp.maximum(entries, -bound), bound).astype(kind)


def bell_draw_with(key, extent, width, limit, shards, heavy, kind=jnp.bfloat16):
    values = width * jax.random.normal(key, extent, jnp.float32)
    if shards:
        values = values * block_scale(key, extent, shards, -0.22, 0.18)
    return jnp.clip(with_spikes(values, jax.random.fold_in(key, 3), *heavy), -limit, limit).astype(kind)


def setup_inputs(seed: int = 0) -> dict:
    key_list = jax.random.split(jax.random.key(seed), 7)
    return {
        "search_dir": gaussian(key_list[0], (VARS, LEVELS, NY, NX), 1.0, 6.0, ((1, 8), (2, 64)), jnp.float32),
        "perturb": bell_draw_with(key_list[1], (VARS, LEVELS, MEMBERS, NY, NX), 1.0, 6.0, ((2, 8), (3, 64)), (2, 1, 8, 2.0)),
        "smooth_y": draw_smooth_y(jax.random.fold_in(key_list[6], 71), 0),
        "smooth_x": draw_smooth_x(jax.random.fold_in(key_list[6], 71), 0),
        "vertical": draw_vertical(jax.random.fold_in(key_list[6], 71), 0),
        "level_scale": draw_level_scale(jax.random.fold_in(key_list[6], 71), 0),
    }


def power_stack(matrix):
    highest = lax.Precision.HIGHEST
    power = jnp.eye(matrix.shape[0], dtype=jnp.float32)
    result = []
    for step in range(PMAX):
        power = jnp.dot(matrix, power, precision=highest)
        result.append(jnp.dot(power, power.T, precision=highest))
    return jnp.stack(result)


def reference(search_dir, perturb, smooth_y, smooth_x, vertical, level_scale):
    highest = lax.Precision.HIGHEST
    stack_y = power_stack(smooth_y)
    stack_x = power_stack(smooth_x)
    pick_y = jnp.take(stack_y, (level_scale - 1).astype(jnp.int32), axis=0)
    pick_x = jnp.take(stack_x, (level_scale - 1).astype(jnp.int32), axis=0)

    def member(total, index):
        field = jnp.take(perturb, index, axis=2).astype(jnp.float32)
        controls = jnp.sum(field * search_dir, axis=0)
        adjoint = jnp.einsum("ql,qyx->lyx", vertical, controls, precision=highest)
        smoothed = jnp.einsum("lij,ljx->lix", pick_y, adjoint, precision=highest)
        smoothed = jnp.einsum("lyj,ljx->lyx", smoothed, pick_x, precision=highest)
        forward = jnp.einsum("lq,qyx->lyx", vertical, smoothed, precision=highest)
        return total + field * forward[None], None

    start = jnp.zeros(search_dir.shape, jnp.float32)
    total, unused = lax.scan(member, start, jnp.arange(MEMBERS, dtype=jnp.int32))
    return total / (MEMBERS - 1)
```

```python
import jax
import jax.numpy as jnp
from jax import lax
from jax.experimental import pallas as pl
from jax.experimental.pallas import tpu as pltpu
from jax.sharding import PartitionSpec as P

F32 = jnp.float32
BF16 = jnp.bfloat16
VMEM_LIMIT = 50 * 1024 * 1024
LEVELS = 64
VARS = 5
ROWS = 64
CHUNK = 16
STEPS = ROWS // CHUNK


def split(value):
    high = value.astype(BF16)
    low = (value - high.astype(F32)).astype(BF16)
    return high, low


def dot(a, b):
    return jnp.dot(a, b, preferred_element_type=F32)


def vertical_product(matrix, source, target):
    m_high, m_low = split(matrix)
    left = jnp.concatenate([m_high, m_high, m_low], axis=1)
    for pair in range(CHUNK // 2):
        parts = [source[pl.ds(2 * pair + i, LEVELS, stride=CHUNK), :] for i in range(2)]
        high, low = split(jnp.concatenate(parts, axis=1))
        result = dot(left, jnp.concatenate([high, low, high], axis=0))
        for i in range(2):
            target[pl.ds(2 * pair + i, LEVELS, stride=CHUNK), :] = result[:, 128 * i : 128 * (i + 1)]


def adjoint_kernel(dir_ref, perturb_ref, matrix_ref, out_ref, controls, result):
    def level(q, carry):
        total = None
        for v in range(VARS):
            direction = dir_ref[v, q]
            direction = jnp.concatenate([direction] * (CHUNK // 4), axis=0)
            term = perturb_ref[v, q].astype(F32) * direction
            total = term if total is None else total + term
        controls[pl.ds(pl.multiple_of(q * CHUNK, CHUNK), CHUNK), :] = total
        return carry

    lax.fori_loop(0, LEVELS, level, 0, unroll=4)
    vertical_product(matrix_ref[...], controls, result)
    out_ref[...] = result[...].reshape(LEVELS, CHUNK, 128)


def prepare_kernel(scale_ref, smooth_y_ref, smooth_x_ref, y_ref, xh_ref, xl_ref):
    scale = scale_ref[0]

    def covariance(matrix):
        power = matrix
        chosen = matrix
        for step in range(2, 5):
            power = jnp.dot(matrix, power, precision=lax.Precision.HIGHEST, preferred_element_type=F32)
            chosen = jnp.where(scale == step, power, chosen)
        return lax.dot_general(
            chosen, chosen, (((1,), (1,)), ((), ())), precision=lax.Precision.HIGHEST, preferred_element_type=F32
        )

    high, low = split(covariance(smooth_y_ref[...]))
    y_ref[...] = jnp.concatenate([high, high, low], axis=1)
    high, low = split(covariance(smooth_x_ref[...]))
    xh_ref[...] = high
    xl_ref[...] = low


def smooth_kernel(in_ref, y_ref, xh_ref, xl_ref, out_ref, source, target):
    source[...] = in_ref[...].reshape(LEVELS * CHUNK, 128)
    xh, xl = xh_ref[...], xl_ref[...]
    y_both, y_low = y_ref[:, :256], y_ref[:, 256:]
    for k in range(CHUNK // 4):
        halves = []
        for r in range(2):
            parts = [source[pl.ds(4 * k + 2 * half + r, LEVELS, stride=CHUNK), :] for half in range(2)]
            halves.append(jnp.concatenate(parts, axis=1))
        high, low = split(jnp.concatenate(halves, axis=0))
        along_x = dot(high, xh) + dot(low, xh) + dot(high, xl)
        high, low = split(along_x)
        result = dot(y_both, jnp.concatenate([high, low], axis=0)) + dot(y_low, high)
        for r in range(2):
            for half in range(2):
                target[pl.ds(4 * k + 2 * half + r, LEVELS, stride=CHUNK), :] = result[
                    64 * r : 64 * (r + 1), 128 * half : 128 * (half + 1)
                ]
    out_ref[...] = target[...].reshape(LEVELS, CHUNK, 128)


def increment_kernel(place_ref, in_ref, perturb_ref, matrix_ref, give_ref, keep_ref, source, forward, total):
    step = pl.program_id(0)
    source[...] = in_ref[...].reshape(LEVELS * CHUNK, 128)
    vertical_product(matrix_ref[...], source, forward)

    @pl.when(step == 0)
    def _():
        total[...] = jnp.zeros_like(total)

    def level(q, carry):
        field = forward[pl.ds(pl.multiple_of(q * CHUNK, CHUNK), CHUNK), :]
        for v in range(VARS):
            term = perturb_ref[v, q].astype(F32) * field
            total[v, q] += term[:8] + term[8:]
        return carry

    lax.fori_loop(0, LEVELS, level, 0, unroll=4)

    @pl.when(step == STEPS - 1)
    def _():
        chip, core = place_ref[0], place_ref[1]
        for j in range(4):
            block = lax.rem(chip + j, 4) * 16
            for ref, parity in ((keep_ref, core), (give_ref, 1 - core)):

                def fold(i, carry, ref=ref, base=block + 8 * parity, j=j):
                    for v in range(VARS):
                        both = total[v, base + i]
                        ref[j, v, i] = both[:4] + both[4:]
                    return carry

                lax.fori_loop(0, 8, fold, 0)


def whole(shape):
    return pl.BlockSpec(shape, lambda i: (0,) * len(shape))


PERTURB_BLOCK = pl.BlockSpec((VARS, LEVELS, CHUNK, 128), lambda i: (0, 0, i, 0))
FIELD_BLOCK = pl.BlockSpec((LEVELS, CHUNK, 128), lambda i: (0, i, 0))
FIELDS = jax.ShapeDtypeStruct((LEVELS, ROWS, 128), F32)
FIELD_SCRATCH = pltpu.VMEM((LEVELS * CHUNK, 128), F32)
PARAMS = pltpu.CompilerParams(vmem_limit_bytes=VMEM_LIMIT)


def to_lines(array):
    lead = array.shape[:-2]
    n = len(lead)
    array = array.reshape(lead + (2, 2, 128))
    return array.transpose(tuple(range(n)) + (n + 1, n, n + 2)).reshape(lead + (4, 128))


def per_device(search_dir, perturb, smooth_y, smooth_x, vertical, level_scale):
    mem = lax.axis_index("mem")
    chip, core = mem // 2, mem % 2
    lines = to_lines(perturb).reshape(VARS, LEVELS, ROWS, 128)
    full_dir = lax.all_gather(to_lines(search_dir), "mem", axis=1, tiled=True)
    adjoint = pl.pallas_call(
        adjoint_kernel,
        grid=(STEPS,),
        in_specs=[whole((VARS, LEVELS, 4, 128)), PERTURB_BLOCK, whole((64, 64))],
        out_specs=FIELD_BLOCK,
        out_shape=FIELDS,
        scratch_shapes=[FIELD_SCRATCH, FIELD_SCRATCH],
        compiler_params=PARAMS,
        cost_estimate=pl.CostEstimate(flops=200_000_000, bytes_accessed=8_000_000, transcendentals=0),
        name="adjoint",
    )(full_dir, lines, vertical.T)

    scale = lax.dynamic_slice_in_dim(level_scale, lax.axis_index("tile"), 1)
    ordered_y = smooth_y.reshape(64, 2, 64, 2).transpose(1, 0, 3, 2).reshape(128, 128)
    vmem = pl.BlockSpec(memory_space=pltpu.VMEM)
    cov_y, cov_xh, cov_xl = pl.pallas_call(
        prepare_kernel,
        in_specs=[pl.BlockSpec(memory_space=pltpu.SMEM), vmem, vmem],
        out_specs=[vmem, vmem, vmem],
        out_shape=[
            jax.ShapeDtypeStruct((128, 384), BF16),
            jax.ShapeDtypeStruct((256, 256), BF16),
            jax.ShapeDtypeStruct((256, 256), BF16),
        ],
        compiler_params=PARAMS,
        cost_estimate=pl.CostEstimate(flops=1_000_000_000, bytes_accessed=1_000_000, transcendentals=0),
        name="prepare",
    )(scale, ordered_y, smooth_x)

    owned = lax.all_to_all(adjoint, "tile", split_axis=0, concat_axis=0, tiled=True)
    smoothed = pl.pallas_call(
        smooth_kernel,
        grid=(STEPS,),
        in_specs=[FIELD_BLOCK, whole((128, 384)), whole((256, 256)), whole((256, 256))],
        out_specs=FIELD_BLOCK,
        out_shape=FIELDS,
        scratch_shapes=[FIELD_SCRATCH, FIELD_SCRATCH],
        compiler_params=PARAMS,
        cost_estimate=pl.CostEstimate(flops=1_200_000_000, bytes_accessed=4_000_000, transcendentals=0),
        name="smooth",
    )(owned, cov_y, cov_xh, cov_xl)
    returned = lax.all_to_all(smoothed, "tile", split_axis=0, concat_axis=0, tiled=True)

    share = jax.ShapeDtypeStruct((4, VARS, 8, 4, 128), F32)
    give, keep = pl.pallas_call(
        increment_kernel,
        grid=(STEPS,),
        in_specs=[pl.BlockSpec(memory_space=pltpu.SMEM), FIELD_BLOCK, PERTURB_BLOCK, whole((64, 64))],
        out_specs=[whole(share.shape), whole(share.shape)],
        out_shape=[share, share],
        scratch_shapes=[FIELD_SCRATCH, FIELD_SCRATCH, pltpu.VMEM((VARS, LEVELS, 8, 128), F32)],
        compiler_params=PARAMS,
        cost_estimate=pl.CostEstimate(flops=200_000_000, bytes_accessed=8_000_000, transcendentals=0),
        name="increment",
    )(jnp.stack([chip, core]), returned, lines, vertical)

    other = lax.ppermute(give, "mem", [(m, m ^ 1) for m in range(8)])
    pieces = [keep[j] + other[j] for j in range(4)]
    total = pieces[0]
    for j in (2, 1, 3):
        total = total + lax.ppermute(pieces[j], "mem", [(m, (m + 2 * j) % 8) for m in range(8)])
    total = total / (128 - 1)
    total = total.reshape(VARS, 8, 2, 2, 128).transpose(0, 1, 3, 2, 4)
    return total.reshape(VARS, 8, 2, 256)


def solution(mesh):
    in_specs = (
        P(None, "mem", "tile", None),
        P(None, None, "mem", "tile", None),
        P(),
        P(),
        P(),
        P(),
    )
    out_specs = P(None, "mem", "tile", None)
    return jax.shard_map(
        per_device, mesh=mesh, in_specs=in_specs, out_specs=out_specs, check_vma=False
    )
```

```python
import jax
import jax.numpy as jnp
from jax import lax
from jax.experimental import pallas as pl
from jax.experimental.pallas import tpu as pltpu
from jax.sharding import PartitionSpec as P

F32 = jnp.float32
BF16 = jnp.bfloat16
LEVELS = 64
VARS = 5
ROWS = 64
PITCH = 72
GROUP = 8


def split(value):
    high = value.astype(BF16)
    low = (value - high.astype(F32)).astype(BF16)
    return high, low


def dot(a, b):
    return jnp.dot(a, b, preferred_element_type=F32)


def every_level(row):
    return pl.ds(row, LEVELS, stride=PITCH)


def level_rows(level):
    return pl.ds(pl.multiple_of(level * PITCH, 8), ROWS)


def spread(source, target):
    for level in range(LEVELS):
        target[level * PITCH : level * PITCH + ROWS, :] = source[level * ROWS : (level + 1) * ROWS, :]


def vertical_product(matrix, source, target, after=lambda step: None):
    m_high, m_low = split(matrix)
    zero = jnp.zeros_like(m_high)
    left = jnp.concatenate(
        [jnp.concatenate([m_high, m_high], axis=1), jnp.concatenate([m_low, zero], axis=1)], axis=0
    )

    def half(step, carry):
        for pair in range(ROWS // 4):
            first = step * (ROWS // 2) + 2 * pair
            parts = [source[every_level(first + i), :] for i in range(2)]
            high, low = split(jnp.concatenate(parts, axis=1))
            result = dot(left, jnp.concatenate([high, low], axis=0))
            result = result[:LEVELS] + result[LEVELS:]
            for i in range(2):
                target[every_level(first + i), :] = result[:, 128 * i : 128 * (i + 1)]
            if pair % (GROUP // 2) == GROUP // 2 - 1:
                after(step * (ROWS // 2 // GROUP) + pair // (GROUP // 2))
        return carry

    lax.fori_loop(0, 2, half, 0)


def send_rows(result, out_ref, sem, step):
    rows = pl.ds(pl.multiple_of(step * GROUP, GROUP), GROUP)
    view = result.reshape(LEVELS, PITCH, 128)
    return pltpu.make_async_copy(view.at[:, rows], out_ref.at[:, rows], sem.at[step])


def wait_rows(result, out_ref, sem):
    for step in range(ROWS // GROUP):
        send_rows(result, out_ref, sem, step).wait()


def adjoint_kernel(dir_ref, perturb_ref, matrix_ref, out_ref, lines, controls, result, in_sem, out_sem):
    pieces = []
    for c in range(8):
        part = pl.ds(8 * c, 8)
        pieces.append(pltpu.make_async_copy(perturb_ref.at[:, part], lines.at[:, part], in_sem.at[c]))
        pieces[c].start()

    def level(q, carry):
        total = None
        for v in range(VARS):
            direction = dir_ref[v, q]
            direction = jnp.concatenate([direction, direction], axis=0)
            term = lines[v, q].astype(F32).reshape(ROWS // 8, 8, 128) * direction[None]
            total = term if total is None else total + term
        controls[level_rows(q), :] = total.reshape(ROWS, 128)
        return carry

    for c in range(8):
        pieces[c].wait()
        lax.fori_loop(8 * c, 8 * c + 8, level, 0, unroll=2)
    vertical_product(
        matrix_ref[...].T, controls, result, lambda step: send_rows(result, out_ref, out_sem, step).start()
    )
    wait_rows(result, out_ref, out_sem)


def prepare_kernel(scale_ref, smooth_y_ref, smooth_x_ref, y_ref, xh_ref, xl_ref):
    scale = scale_ref[0]

    def covariance(matrix):
        power = matrix
        chosen = matrix
        for step in range(2, 5):
            power = jnp.dot(matrix, power, precision=lax.Precision.HIGHEST, preferred_element_type=F32)
            chosen = jnp.where(scale == step, power, chosen)
        return lax.dot_general(
            chosen, chosen, (((1,), (1,)), ((), ())), precision=lax.Precision.HIGHEST, preferred_element_type=F32
        )

    high, low = split(covariance(smooth_y_ref[...]))
    y_ref[...] = jnp.concatenate([high, high, low], axis=1)
    high, low = split(covariance(smooth_x_ref[...]))
    xh_ref[...] = high
    xl_ref[...] = low


def smooth_kernel(in_ref, y_ref, xh_ref, xl_ref, out_ref, source, result, out_sem):
    xh, xl = xh_ref[...], xl_ref[...]
    y_both, y_low = y_ref[:, :256], y_ref[:, 256:]
    spread(in_ref, source)

    def member(k):
        halves = []
        for r in range(2):
            parts = [source[every_level(4 * k + 2 * half + r), :] for half in range(2)]
            halves.append(jnp.concatenate(parts, axis=1))
        high, low = split(jnp.concatenate(halves, axis=0))
        along_x = dot(high, xh) + dot(low, xh) + dot(high, xl)
        high, low = split(along_x)
        smoothed = dot(y_both, jnp.concatenate([high, low], axis=0)) + dot(y_low, high)
        for r in range(2):
            for half in range(2):
                result[every_level(4 * k + 2 * half + r), :] = smoothed[
                    64 * r : 64 * (r + 1), 128 * half : 128 * (half + 1)
                ]

    def group(step, carry):
        for k in range(4):
            member(step * 4 + k)
            if k % 2:
                send_rows(result, out_ref, out_sem, step * 2 + k // 2).start()
        return carry

    lax.fori_loop(0, 4, group, 0)
    wait_rows(result, out_ref, out_sem)


def fetch_levels(parity, perturb_ref, lines, sem):
    pieces = []
    for chip in range(4):
        part = pl.ds(chip * 16 + parity * 8, 8)
        pieces.append(pltpu.make_async_copy(perturb_ref.at[:, part], lines.at[chip], sem.at[chip]))
        pieces[chip].start()
    return pieces


def increment_terms(parity, pieces, lines, forward_ref, out_ref):
    for chip in range(4):
        pieces[chip].wait()

        def level(i, carry, chip=chip):
            field = forward_ref[level_rows(chip * 16 + parity * 8 + i), :]
            for v in range(VARS):
                terms = lines[chip, v, i].astype(F32) * field
                eight = jnp.sum(terms.reshape(ROWS // 8, 8, 128), axis=0)
                out_ref[chip, v, i] = eight[:4] + eight[4:]
            return carry

        lax.fori_loop(0, 8, level, 0, unroll=2)


def give_kernel(core_ref, in_ref, perturb_ref, matrix_ref, forward_ref, give_ref, lines, source, sem):
    parity = 1 - core_ref[0]
    pieces = fetch_levels(parity, perturb_ref, lines, sem)
    spread(in_ref, source)
    vertical_product(matrix_ref[...], source, forward_ref)
    increment_terms(parity, pieces, lines, forward_ref, give_ref)


def keep_kernel(core_ref, forward_ref, perturb_ref, keep_ref, lines, sem):
    parity = core_ref[0]
    pieces = fetch_levels(parity, perturb_ref, lines, sem)
    increment_terms(parity, pieces, lines, forward_ref, keep_ref)


def finish_kernel(in_ref, out_ref):
    total = (in_ref[0] + in_ref[1]) + (in_ref[2] + in_ref[3])
    out_ref[...] = total / (128 - 1)


VMEM = pl.BlockSpec(memory_space=pltpu.VMEM)
SMEM = pl.BlockSpec(memory_space=pltpu.SMEM)
HBM = pl.BlockSpec(memory_space=pltpu.HBM)
FIELDS = jax.ShapeDtypeStruct((LEVELS, ROWS, 128), F32)
FLAT = jax.ShapeDtypeStruct((LEVELS * ROWS, 128), F32)
SHARE = jax.ShapeDtypeStruct((4, VARS, 8, 4, 128), F32)
SPREAD = jax.ShapeDtypeStruct((LEVELS * PITCH, 128), F32)
SPREAD_SCRATCH = pltpu.VMEM(SPREAD.shape, F32)
HALF_SCRATCH = pltpu.VMEM((4, VARS, 8, ROWS, 128), BF16)
DMA = pltpu.SemaphoreType.DMA


def call(kernel, name, in_specs, out, flops, scratch=(), vmem=24):
    return pl.pallas_call(
        kernel,
        in_specs=in_specs,
        out_specs=[spec for spec, shape in out] if len(out) > 1 else out[0][0],
        out_shape=[shape for spec, shape in out] if len(out) > 1 else out[0][1],
        scratch_shapes=list(scratch),
        compiler_params=pltpu.CompilerParams(vmem_limit_bytes=vmem * 1024 * 1024),
        cost_estimate=pl.CostEstimate(flops=flops, bytes_accessed=4_000_000, transcendentals=0),
        name=name,
    )


adjoint_call = call(
    adjoint_kernel,
    "adjoint",
    [VMEM, HBM, VMEM],
    [(HBM, FIELDS)],
    300_000_000,
    [pltpu.VMEM((VARS, LEVELS, ROWS, 128), BF16), SPREAD_SCRATCH, SPREAD_SCRATCH, DMA((8,)), DMA((8,))],
    vmem=60,
)
prepare_call = call(
    prepare_kernel,
    "prepare",
    [SMEM, VMEM, VMEM],
    [
        (VMEM, jax.ShapeDtypeStruct((128, 384), BF16)),
        (VMEM, jax.ShapeDtypeStruct((256, 256), BF16)),
        (VMEM, jax.ShapeDtypeStruct((256, 256), BF16)),
    ],
    1_000_000_000,
)
smooth_call = call(
    smooth_kernel,
    "smooth",
    [VMEM] * 4,
    [(HBM, FIELDS)],
    1_200_000_000,
    [SPREAD_SCRATCH, SPREAD_SCRATCH, DMA((8,))],
    vmem=48,
)
give_call = call(
    give_kernel,
    "give",
    [SMEM, VMEM, HBM, VMEM],
    [(VMEM, SPREAD), (VMEM, SHARE)],
    300_000_000,
    [HALF_SCRATCH, SPREAD_SCRATCH, DMA((4,))],
    vmem=48,
)
keep_call = call(
    keep_kernel,
    "keep",
    [SMEM, VMEM, HBM],
    [(VMEM, SHARE)],
    100_000_000,
    [HALF_SCRATCH, DMA((4,))],
    vmem=48,
)
finish_call = call(
    finish_kernel, "finish", [VMEM], [(VMEM, jax.ShapeDtypeStruct((VARS, 8, 4, 128), F32))], 1_000_000
)


def to_lines(array):
    lead = array.shape[:-2]
    n = len(lead)
    array = array.reshape(lead + (2, 2, 128))
    return array.transpose(tuple(range(n)) + (n + 1, n, n + 2)).reshape(lead + (4, 128))


def exchange(fields):
    return lax.all_to_all(fields, "tile", split_axis=0, concat_axis=0, tiled=True)


def flat(fields):
    return fields.reshape(FLAT.shape)


def per_device(search_dir, perturb, smooth_y, smooth_x, vertical, level_scale):
    core = lax.rem(lax.axis_index("mem"), 2)[None]
    lines = to_lines(perturb).reshape(VARS, LEVELS, ROWS, 128)
    full_dir = lax.all_gather(to_lines(search_dir), "mem", axis=1, tiled=True)
    adjoint = adjoint_call(full_dir, lines, vertical)

    scale = lax.dynamic_slice_in_dim(level_scale, lax.axis_index("tile"), 1)
    ordered_y = smooth_y.reshape(64, 2, 64, 2).transpose(1, 0, 3, 2).reshape(128, 128)
    cov_y, cov_xh, cov_xl = prepare_call(scale, ordered_y, smooth_x)

    smoothed = smooth_call(flat(exchange(adjoint)), cov_y, cov_xh, cov_xl)
    forward, give = give_call(core, flat(exchange(smoothed)), lines, vertical)
    keep = keep_call(core, forward, lines)
    both = keep + lax.ppermute(give, "mem", [(m, m ^ 1) for m in range(8)])
    both = lax.all_to_all(
        both, "mem", split_axis=0, concat_axis=0, tiled=True, axis_index_groups=[[0, 2, 4, 6], [1, 3, 5, 7]]
    )
    total = finish_call(both).reshape(VARS, 8, 2, 2, 128).transpose(0, 1, 3, 2, 4)
    return total.reshape(VARS, 8, 2, 256)


def solution(mesh):
    in_specs = (
        P(None, "mem", "tile", None),
        P(None, None, "mem", "tile", None),
        P(),
        P(),
        P(),
        P(),
    )
    out_specs = P(None, "mem", "tile", None)
    return jax.shard_map(
        per_device, mesh=mesh, in_specs=in_specs, out_specs=out_specs, check_vma=False
    )
```

```python
import jax
import jax.numpy as jnp
from jax import lax
from jax.experimental import pallas as pl
from jax.experimental.pallas import tpu as pltpu
from jax.sharding import PartitionSpec as P

F32 = jnp.float32
BF16 = jnp.bfloat16
LEVELS = 64
VARS = 5
ROWS = 64
PITCH = 72
GROUP = 8
MEMBERS_AT_ONCE = 4


def split(value):
    high = value.astype(BF16)
    low = (value - high.astype(F32)).astype(BF16)
    return high, low


def dot(a, b):
    return jnp.dot(a, b, preferred_element_type=F32)


def every_level(row):
    return pl.ds(row, LEVELS, stride=PITCH)


def level_rows(level):
    return pl.ds(pl.multiple_of(level * PITCH, 8), ROWS)


def spread(source, target):
    for level in range(LEVELS):
        target[level * PITCH : level * PITCH + ROWS, :] = source[level * ROWS : (level + 1) * ROWS, :]


def vertical_product(matrix, source, target, after=lambda step: None):
    m_high, m_low = split(matrix)
    zero = jnp.zeros_like(m_high)
    left = jnp.concatenate(
        [jnp.concatenate([m_high, m_high], axis=1), jnp.concatenate([m_low, zero], axis=1)], axis=0
    )

    def half(step, carry):
        for pair in range(ROWS // 4):
            first = step * (ROWS // 2) + 2 * pair
            parts = [source[every_level(first + i), :] for i in range(2)]
            high, low = split(jnp.concatenate(parts, axis=1))
            result = dot(left, jnp.concatenate([high, low], axis=0))
            result = result[:LEVELS] + result[LEVELS:]
            for i in range(2):
                target[every_level(first + i), :] = result[:, 128 * i : 128 * (i + 1)]
            if pair % (GROUP // 2) == GROUP // 2 - 1:
                after(step * (ROWS // 2 // GROUP) + pair // (GROUP // 2))
        return carry

    lax.fori_loop(0, 2, half, 0)


def send_rows(result, out_ref, sem, step, count=GROUP):
    rows = pl.ds(pl.multiple_of(step * count, GROUP), count)
    view = result.reshape(LEVELS, PITCH, 128)
    return pltpu.make_async_copy(view.at[:, rows], out_ref.at[:, rows], sem.at[step])


def wait_rows(result, out_ref, sem, count=GROUP):
    for step in range(ROWS // count):
        send_rows(result, out_ref, sem, step, count).wait()


def adjoint_kernel(dir_ref, perturb_ref, matrix_ref, out_ref, lines, controls, result, in_sem, out_sem):
    pieces = []
    for c in range(8):
        part = pl.ds(8 * c, 8)
        pieces.append(pltpu.make_async_copy(perturb_ref.at[:, part], lines.at[:, part], in_sem.at[c]))
        pieces[c].start()

    def level(q, carry):
        total = None
        for v in range(VARS):
            direction = dir_ref[v, q]
            direction = jnp.concatenate([direction, direction], axis=0)
            term = lines[v, q].astype(F32).reshape(ROWS // 8, 8, 128) * direction[None]
            total = term if total is None else total + term
        controls[level_rows(q), :] = total.reshape(ROWS, 128)
        return carry

    for c in range(8):
        pieces[c].wait()
        lax.fori_loop(8 * c, 8 * c + 8, level, 0, unroll=2)
    vertical_product(
        matrix_ref[...].T, controls, result, lambda step: send_rows(result, out_ref, out_sem, step).start()
    )
    wait_rows(result, out_ref, out_sem)


def prepare_kernel(scale_ref, smooth_y_ref, smooth_x_ref, y_ref, xh_ref, xl_ref):
    scale = scale_ref[0]

    def covariance(matrix):
        power = matrix
        chosen = matrix
        for step in range(2, 5):
            power = jnp.dot(matrix, power, precision=lax.Precision.HIGHEST, preferred_element_type=F32)
            chosen = jnp.where(scale == step, power, chosen)
        return lax.dot_general(
            chosen, chosen, (((1,), (1,)), ((), ())), precision=lax.Precision.HIGHEST, preferred_element_type=F32
        )

    high, low = split(covariance(smooth_y_ref[...]))
    y_ref[...] = jnp.concatenate([high, high, low], axis=1)
    high, low = split(covariance(smooth_x_ref[...]))
    xh_ref[...] = high
    xl_ref[...] = low


def smooth_kernel(in_ref, y_ref, xh_ref, xl_ref, spent_ref, out_ref, source, result, out_sem):
    del spent_ref
    xh, xl = xh_ref[...], xl_ref[...]
    y_both, y_low = y_ref[:, :256], y_ref[:, 256:]
    spread(in_ref, source)
    for step in range(ROWS // 4 // MEMBERS_AT_ONCE):
        first = step * MEMBERS_AT_ONCE * 4
        halves = []
        for k in range(MEMBERS_AT_ONCE):
            for r in range(2):
                parts = [source[every_level(first + 4 * k + 2 * half + r), :] for half in range(2)]
                halves.append(jnp.concatenate(parts, axis=1))
        high, low = split(jnp.concatenate(halves, axis=0))
        along_x = dot(high, xh) + dot(low, xh) + dot(high, xl)
        for k in range(MEMBERS_AT_ONCE):
            high, low = split(along_x[128 * k : 128 * (k + 1)])
            smoothed = dot(y_both, jnp.concatenate([high, low], axis=0)) + dot(y_low, high)
            for r in range(2):
                for half in range(2):
                    result[every_level(first + 4 * k + 2 * half + r), :] = smoothed[
                        64 * r : 64 * (r + 1), 128 * half : 128 * (half + 1)
                    ]
        send_rows(result, out_ref, out_sem, step, 4 * MEMBERS_AT_ONCE).start()
    wait_rows(result, out_ref, out_sem, 4 * MEMBERS_AT_ONCE)


def fetch_levels(parity, perturb_ref, lines, sem):
    pieces = []
    for chip in range(4):
        part = pl.ds(chip * 16 + parity * 8, 8)
        pieces.append(pltpu.make_async_copy(perturb_ref.at[:, part], lines.at[chip], sem.at[chip]))
        pieces[chip].start()
    return pieces


def increment_terms(parity, pieces, lines, forward_ref, out_ref):
    for chip in range(4):
        pieces[chip].wait()

        def level(i, carry, chip=chip):
            field = forward_ref[level_rows(chip * 16 + parity * 8 + i), :]
            for v in range(VARS):
                terms = lines[chip, v, i].astype(F32) * field
                eight = jnp.sum(terms.reshape(ROWS // 8, 8, 128), axis=0)
                out_ref[chip, v, i] = eight[:4] + eight[4:]
            return carry

        lax.fori_loop(0, 8, level, 0, unroll=2)


def give_kernel(core_ref, in_ref, perturb_ref, matrix_ref, forward_ref, give_ref, lines, source, sem):
    parity = 1 - core_ref[0]
    pieces = fetch_levels(parity, perturb_ref, lines, sem)
    spread(in_ref, source)
    vertical_product(matrix_ref[...], source, forward_ref)
    increment_terms(parity, pieces, lines, forward_ref, give_ref)


def keep_kernel(core_ref, forward_ref, perturb_ref, keep_ref, lines, sem):
    parity = core_ref[0]
    pieces = fetch_levels(parity, perturb_ref, lines, sem)
    increment_terms(parity, pieces, lines, forward_ref, keep_ref)


def finish_kernel(in_ref, out_ref):
    total = (in_ref[0] + in_ref[1]) + (in_ref[2] + in_ref[3])
    out_ref[...] = total / (128 - 1)


VMEM = pl.BlockSpec(memory_space=pltpu.VMEM)
SMEM = pl.BlockSpec(memory_space=pltpu.SMEM)
HBM = pl.BlockSpec(memory_space=pltpu.HBM)
FIELDS = jax.ShapeDtypeStruct((LEVELS, ROWS, 128), F32)
FLAT = jax.ShapeDtypeStruct((LEVELS * ROWS, 128), F32)
SHARE = jax.ShapeDtypeStruct((4, VARS, 8, 4, 128), F32)
SPREAD = jax.ShapeDtypeStruct((LEVELS * PITCH, 128), F32)
SPREAD_SCRATCH = pltpu.VMEM(SPREAD.shape, F32)
HALF_SCRATCH = pltpu.VMEM((4, VARS, 8, ROWS, 128), BF16)
DMA = pltpu.SemaphoreType.DMA


def call(kernel, name, in_specs, out, flops, scratch=(), vmem=24, aliases=None):
    return pl.pallas_call(
        kernel,
        in_specs=in_specs,
        out_specs=[spec for spec, shape in out] if len(out) > 1 else out[0][0],
        out_shape=[shape for spec, shape in out] if len(out) > 1 else out[0][1],
        scratch_shapes=list(scratch),
        input_output_aliases=aliases or {},
        compiler_params=pltpu.CompilerParams(vmem_limit_bytes=vmem * 1024 * 1024),
        cost_estimate=pl.CostEstimate(flops=flops, bytes_accessed=4_000_000, transcendentals=0),
        name=name,
    )


adjoint_call = call(
    adjoint_kernel,
    "adjoint",
    [VMEM, HBM, VMEM],
    [(HBM, FIELDS)],
    300_000_000,
    [pltpu.VMEM((VARS, LEVELS, ROWS, 128), BF16), SPREAD_SCRATCH, SPREAD_SCRATCH, DMA((8,)), DMA((8,))],
    vmem=60,
)
prepare_call = call(
    prepare_kernel,
    "prepare",
    [SMEM, VMEM, VMEM],
    [
        (VMEM, jax.ShapeDtypeStruct((128, 384), BF16)),
        (VMEM, jax.ShapeDtypeStruct((256, 256), BF16)),
        (VMEM, jax.ShapeDtypeStruct((256, 256), BF16)),
    ],
    1_000_000_000,
)
smooth_call = call(
    smooth_kernel,
    "smooth",
    [VMEM] * 4 + [HBM],
    [(HBM, FIELDS)],
    1_200_000_000,
    [SPREAD_SCRATCH, SPREAD_SCRATCH, DMA((4,))],
    vmem=48,
    aliases={4: 0},
)
give_call = call(
    give_kernel,
    "give",
    [SMEM, VMEM, HBM, VMEM],
    [(VMEM, SPREAD), (VMEM, SHARE)],
    300_000_000,
    [HALF_SCRATCH, SPREAD_SCRATCH, DMA((4,))],
    vmem=48,
)
keep_call = call(
    keep_kernel,
    "keep",
    [SMEM, VMEM, HBM],
    [(VMEM, SHARE)],
    100_000_000,
    [HALF_SCRATCH, DMA((4,))],
    vmem=48,
)
finish_call = call(
    finish_kernel, "finish", [VMEM], [(VMEM, jax.ShapeDtypeStruct((VARS, 8, 4, 128), F32))], 1_000_000
)


def to_lines(array):
    lead = array.shape[:-2]
    n = len(lead)
    array = array.reshape(lead + (2, 2, 128))
    return array.transpose(tuple(range(n)) + (n + 1, n, n + 2)).reshape(lead + (4, 128))


def exchange(fields):
    return lax.all_to_all(fields, "tile", split_axis=0, concat_axis=0, tiled=True)


def flat(fields):
    return fields.reshape(FLAT.shape)


def per_device(search_dir, perturb, smooth_y, smooth_x, vertical, level_scale):
    core = lax.rem(lax.axis_index("mem"), 2)[None]
    lines = to_lines(perturb).reshape(VARS, LEVELS, ROWS, 128)
    full_dir = lax.all_gather(to_lines(search_dir), "mem", axis=1, tiled=True)
    adjoint = adjoint_call(full_dir, lines, vertical)

    scale = lax.dynamic_slice_in_dim(level_scale, lax.axis_index("tile"), 1)
    ordered_y = smooth_y.reshape(64, 2, 64, 2).transpose(1, 0, 3, 2).reshape(128, 128)
    cov_y, cov_xh, cov_xl = prepare_call(scale, ordered_y, smooth_x)

    smoothed = smooth_call(flat(exchange(adjoint)), cov_y, cov_xh, cov_xl, adjoint)
    forward, give = give_call(core, flat(exchange(smoothed)), lines, vertical)
    keep = keep_call(core, forward, lines)
    both = keep + lax.ppermute(give, "mem", [(m, m ^ 1) for m in range(8)])
    both = lax.all_to_all(
        both, "mem", split_axis=0, concat_axis=0, tiled=True, axis_index_groups=[[0, 2, 4, 6], [1, 3, 5, 7]]
    )
    total = finish_call(both).reshape(VARS, 8, 2, 2, 128).transpose(0, 1, 3, 2, 4)
    return total.reshape(VARS, 8, 2, 256)


def solution(mesh):
    in_specs = (
        P(None, "mem", "tile", None),
        P(None, None, "mem", "tile", None),
        P(),
        P(),
        P(),
        P(),
    )
    out_specs = P(None, "mem", "tile", None)
    return jax.shard_map(
        per_device, mesh=mesh, in_specs=in_specs, out_specs=out_specs, check_vma=False
    )
```

```python
import jax
import jax.numpy as jnp
from jax import lax
from jax.experimental import pallas as pl
from jax.experimental.pallas import tpu as pltpu
from jax.sharding import PartitionSpec as P

F32 = jnp.float32
BF16 = jnp.bfloat16
LEVELS = 64
VARS = 5
ROWS = 64
PITCH = 72
GROUP = 8
MEMBERS_AT_ONCE = 4
WIDE_GROUP = 4 * MEMBERS_AT_ONCE


def split(value):
    high = value.astype(BF16)
    low = (value - high.astype(F32)).astype(BF16)
    return high, low


def dot(a, b):
    return jnp.dot(a, b, preferred_element_type=F32)


def outer(matrix):
    return lax.dot_general(
        matrix, matrix, (((1,), (1,)), ((), ())), precision=lax.Precision.HIGHEST, preferred_element_type=F32
    )


def every_level(row):
    return pl.ds(row, LEVELS, stride=PITCH)


def level_rows(level):
    return pl.ds(pl.multiple_of(level * PITCH, 8), ROWS)


def spread(source, target):
    for level in range(LEVELS):
        target[level * PITCH : level * PITCH + ROWS, :] = source[level * ROWS : (level + 1) * ROWS, :]


def vertical_product(matrix, source, target):
    m_high, m_low = split(matrix)
    zero = jnp.zeros_like(m_high)
    left = jnp.concatenate(
        [jnp.concatenate([m_high, m_high], axis=1), jnp.concatenate([m_low, zero], axis=1)], axis=0
    )

    def half(step, carry):
        for pair in range(ROWS // 4):
            first = step * (ROWS // 2) + 2 * pair
            parts = [source[every_level(first + i), :] for i in range(2)]
            high, low = split(jnp.concatenate(parts, axis=1))
            result = dot(left, jnp.concatenate([high, low], axis=0))
            result = result[:LEVELS] + result[LEVELS:]
            for i in range(2):
                target[every_level(first + i), :] = result[:, 128 * i : 128 * (i + 1)]
        return carry

    lax.fori_loop(0, 2, half, 0)


def send_rows(result, out_ref, sem, step, count=GROUP):
    rows = pl.ds(pl.multiple_of(step * count, GROUP), count)
    view = result.reshape(LEVELS, PITCH, 128)
    return pltpu.make_async_copy(view.at[:, rows], out_ref.at[:, rows], sem.at[step])


def wait_rows(result, out_ref, sem, count=GROUP):
    for step in range(ROWS // count):
        send_rows(result, out_ref, sem, step, count).wait()


def smooth_along_x(scale_ref, smooth_x_ref, fields, x_high, x_low):
    matrix = smooth_x_ref[...]
    power = matrix
    for step in range(4):
        if step:
            power = jnp.dot(matrix, power, precision=lax.Precision.HIGHEST, preferred_element_type=F32)
        high, low = split(outer(power))
        x_high[step] = high
        x_low[step] = low

    def level(q, carry):
        scale = scale_ref[q] - 1
        places = [[pl.ds(q * PITCH + 2 * half + r, ROWS // 4, stride=4) for half in range(2)] for r in range(2)]
        lines = [jnp.concatenate([fields[place, :] for place in pair], axis=1) for pair in places]
        high, low = split(jnp.concatenate(lines, axis=0))
        both = dot(jnp.concatenate([high, low], axis=0), x_high[scale])
        product = both[: ROWS // 2] + both[ROWS // 2 :] + dot(high, x_low[scale])
        for r in range(2):
            for half in range(2):
                fields[places[r][half], :] = product[
                    ROWS // 4 * r : ROWS // 4 * (r + 1), 128 * half : 128 * (half + 1)
                ]
        return carry

    lax.fori_loop(0, LEVELS, level, 0, unroll=4)


def adjoint_kernel(
    core_ref,
    scale_ref,
    dir_ref,
    perturb_ref,
    matrix_ref,
    smooth_x_ref,
    early_ref,
    out_ref,
    lines,
    controls,
    result,
    x_high,
    x_low,
    in_sem,
    out_sem,
):
    del early_ref
    pieces = []
    for c in range(8):
        part = pl.ds(8 * c, 8)
        pieces.append(pltpu.make_async_copy(perturb_ref.at[:, part], lines.at[:, part], in_sem.at[c]))
        pieces[c].start()

    def level(q, carry):
        total = None
        for v in range(VARS):
            direction = dir_ref[v, q]
            direction = jnp.concatenate([direction, direction], axis=0)
            term = lines[v, q].astype(F32).reshape(ROWS // 8, 8, 128) * direction[None]
            total = term if total is None else total + term
        controls[level_rows(q), :] = total.reshape(ROWS, 128)
        return carry

    for c in range(8):
        pieces[c].wait()
        lax.fori_loop(8 * c, 8 * c + 8, level, 0, unroll=2)
    vertical_product(matrix_ref[...].T, controls, result)

    @pl.when(core_ref[0] == 1)
    def _():
        smooth_along_x(scale_ref, smooth_x_ref, result, x_high, x_low)

    for step in range(ROWS // WIDE_GROUP):
        send_rows(result, out_ref, out_sem, step, WIDE_GROUP).start()
    wait_rows(result, out_ref, out_sem, WIDE_GROUP)


def chosen_covariance(scale, matrix):
    power = matrix
    chosen = matrix
    for step in range(2, 5):
        power = jnp.dot(matrix, power, precision=lax.Precision.HIGHEST, preferred_element_type=F32)
        chosen = jnp.where(scale == step, power, chosen)
    return split(outer(chosen))


def prepare_y_kernel(scale_ref, smooth_y_ref, y_ref):
    high, low = chosen_covariance(scale_ref[0], smooth_y_ref[...])
    y_ref[...] = jnp.concatenate([high, high, low], axis=1)


def prepare_kernel(scale_ref, smooth_y_ref, smooth_x_ref, y_ref, xh_ref, xl_ref):
    prepare_y_kernel(scale_ref, smooth_y_ref, y_ref)
    high, low = chosen_covariance(scale_ref[0], smooth_x_ref[...])
    xh_ref[...] = high
    xl_ref[...] = low


def smooth_kernel(core_ref, in_ref, y_ref, xh_ref, xl_ref, spent_ref, out_ref, source, result, out_sem):
    del spent_ref
    spread(in_ref, source)

    def run(with_x):
        y_both, y_low = y_ref[:, :256], y_ref[:, 256:]
        for step in range(ROWS // WIDE_GROUP):
            first = step * WIDE_GROUP
            halves = []
            for k in range(MEMBERS_AT_ONCE):
                for r in range(2):
                    parts = [source[every_level(first + 4 * k + 2 * half + r), :] for half in range(2)]
                    halves.append(jnp.concatenate(parts, axis=1))
            fields = jnp.concatenate(halves, axis=0)
            if with_x:
                high, low = split(fields)
                fields = dot(high, xh_ref[...]) + dot(low, xh_ref[...]) + dot(high, xl_ref[...])
            for k in range(MEMBERS_AT_ONCE):
                high, low = split(fields[128 * k : 128 * (k + 1)])
                smoothed = dot(y_both, jnp.concatenate([high, low], axis=0)) + dot(y_low, high)
                for r in range(2):
                    for half in range(2):
                        result[every_level(first + 4 * k + 2 * half + r), :] = smoothed[
                            64 * r : 64 * (r + 1), 128 * half : 128 * (half + 1)
                        ]
            send_rows(result, out_ref, out_sem, step, WIDE_GROUP).start()

    @pl.when(core_ref[0] == 0)
    def _():
        run(True)

    @pl.when(core_ref[0] == 1)
    def _():
        run(False)

    wait_rows(result, out_ref, out_sem, WIDE_GROUP)


def fetch_levels(parity, perturb_ref, lines, sem):
    pieces = []
    for chip in range(4):
        part = pl.ds(chip * 16 + parity * 8, 8)
        pieces.append(pltpu.make_async_copy(perturb_ref.at[:, part], lines.at[chip], sem.at[chip]))
        pieces[chip].start()
    return pieces


def increment_terms(parity, pieces, lines, forward_ref, out_ref):
    for chip in range(4):
        pieces[chip].wait()

        def level(i, carry, chip=chip):
            field = forward_ref[level_rows(chip * 16 + parity * 8 + i), :]
            for v in range(VARS):
                terms = lines[chip, v, i].astype(F32) * field
                eight = jnp.sum(terms.reshape(ROWS // 8, 8, 128), axis=0)
                out_ref[chip, v, i] = eight[:4] + eight[4:]
            return carry

        lax.fori_loop(0, 8, level, 0, unroll=2)


def give_kernel(core_ref, in_ref, perturb_ref, matrix_ref, forward_ref, give_ref, lines, source, sem):
    parity = 1 - core_ref[0]
    pieces = fetch_levels(parity, perturb_ref, lines, sem)
    spread(in_ref, source)
    vertical_product(matrix_ref[...], source, forward_ref)
    increment_terms(parity, pieces, lines, forward_ref, give_ref)


def keep_kernel(core_ref, forward_ref, perturb_ref, keep_ref, lines, sem):
    parity = core_ref[0]
    pieces = fetch_levels(parity, perturb_ref, lines, sem)
    increment_terms(parity, pieces, lines, forward_ref, keep_ref)


def finish_kernel(in_ref, out_ref):
    total = (in_ref[0] + in_ref[1]) + (in_ref[2] + in_ref[3])
    out_ref[...] = total / (128 - 1)


VMEM = pl.BlockSpec(memory_space=pltpu.VMEM)
SMEM = pl.BlockSpec(memory_space=pltpu.SMEM)
HBM = pl.BlockSpec(memory_space=pltpu.HBM)
FIELDS = jax.ShapeDtypeStruct((LEVELS, ROWS, 128), F32)
FLAT = jax.ShapeDtypeStruct((LEVELS * ROWS, 128), F32)
SHARE = jax.ShapeDtypeStruct((4, VARS, 8, 4, 128), F32)
SPREAD = jax.ShapeDtypeStruct((LEVELS * PITCH, 128), F32)
SPREAD_SCRATCH = pltpu.VMEM(SPREAD.shape, F32)
HALF_SCRATCH = pltpu.VMEM((4, VARS, 8, ROWS, 128), BF16)
X_SCRATCH = pltpu.VMEM((4, 256, 256), BF16)
DMA = pltpu.SemaphoreType.DMA


def call(kernel, name, in_specs, out, flops, scratch=(), vmem=24, aliases=None):
    return pl.pallas_call(
        kernel,
        in_specs=in_specs,
        out_specs=[spec for spec, shape in out] if len(out) > 1 else out[0][0],
        out_shape=[shape for spec, shape in out] if len(out) > 1 else out[0][1],
        scratch_shapes=list(scratch),
        input_output_aliases=aliases or {},
        compiler_params=pltpu.CompilerParams(vmem_limit_bytes=vmem * 1024 * 1024),
        cost_estimate=pl.CostEstimate(flops=flops, bytes_accessed=4_000_000, transcendentals=0),
        name=name,
    )


adjoint_call = call(
    adjoint_kernel,
    "adjoint",
    [SMEM, SMEM, VMEM, HBM, VMEM, VMEM, HBM],
    [(HBM, FIELDS)],
    300_000_000,
    [pltpu.VMEM((VARS, LEVELS, ROWS, 128), BF16), SPREAD_SCRATCH, SPREAD_SCRATCH, X_SCRATCH, X_SCRATCH, DMA((8,)), DMA((4,))],
    vmem=60,
)
COV_Y = jax.ShapeDtypeStruct((128, 384), BF16)
COV_X = jax.ShapeDtypeStruct((256, 256), BF16)
prepare_y_call = call(prepare_y_kernel, "prepare_y", [SMEM, VMEM], [(VMEM, COV_Y)], 300_000_000)
prepare_call = call(
    prepare_kernel,
    "prepare",
    [SMEM, VMEM, VMEM],
    [(VMEM, COV_Y), (VMEM, COV_X), (VMEM, COV_X)],
    1_000_000_000,
)
smooth_call = call(
    smooth_kernel,
    "smooth",
    [SMEM] + [VMEM] * 4 + [HBM],
    [(HBM, FIELDS)],
    1_200_000_000,
    [SPREAD_SCRATCH, SPREAD_SCRATCH, DMA((4,))],
    vmem=48,
    aliases={5: 0},
)
give_call = call(
    give_kernel,
    "give",
    [SMEM, VMEM, HBM, VMEM],
    [(VMEM, SPREAD), (VMEM, SHARE)],
    300_000_000,
    [HALF_SCRATCH, SPREAD_SCRATCH, DMA((4,))],
    vmem=48,
)
keep_call = call(
    keep_kernel,
    "keep",
    [SMEM, VMEM, HBM],
    [(VMEM, SHARE)],
    100_000_000,
    [HALF_SCRATCH, DMA((4,))],
    vmem=48,
)
finish_call = call(
    finish_kernel, "finish", [VMEM], [(VMEM, jax.ShapeDtypeStruct((VARS, 8, 4, 128), F32))], 1_000_000
)


def to_lines(array):
    lead = array.shape[:-2]
    n = len(lead)
    array = array.reshape(lead + (2, 2, 128))
    return array.transpose(tuple(range(n)) + (n + 1, n, n + 2)).reshape(lead + (4, 128))


def exchange(fields):
    return lax.all_to_all(fields, "tile", split_axis=0, concat_axis=0, tiled=True)


def flat(fields):
    return fields.reshape(FLAT.shape)


def per_device(search_dir, perturb, smooth_y, smooth_x, vertical, level_scale):
    core = lax.rem(lax.axis_index("mem"), 2)[None]
    lines = to_lines(perturb).reshape(VARS, LEVELS, ROWS, 128)
    full_dir = lax.all_gather(to_lines(search_dir), "mem", axis=1, tiled=True)

    def scale_and_y():
        scale = lax.dynamic_slice_in_dim(level_scale, lax.axis_index("tile"), 1)
        return scale, smooth_y.reshape(64, 2, 64, 2).transpose(1, 0, 3, 2).reshape(128, 128)

    second = core[0] == 1
    early = lax.cond(second, lambda: prepare_y_call(*scale_and_y()), lambda: jnp.zeros(COV_Y.shape, BF16))
    adjoint = adjoint_call(core, level_scale, full_dir, lines, vertical, smooth_x, early)
    cov_y, cov_xh, cov_xl = lax.cond(
        second,
        lambda: [early, jnp.zeros(COV_X.shape, BF16), jnp.zeros(COV_X.shape, BF16)],
        lambda: list(prepare_call(*scale_and_y(), smooth_x)),
    )

    smoothed = smooth_call(core, flat(exchange(adjoint)), cov_y, cov_xh, cov_xl, adjoint)
    forward, give = give_call(core, flat(exchange(smoothed)), lines, vertical)
    keep = keep_call(core, forward, lines)
    both = keep + lax.ppermute(give, "mem", [(m, m ^ 1) for m in range(8)])
    both = lax.all_to_all(
        both, "mem", split_axis=0, concat_axis=0, tiled=True, axis_index_groups=[[0, 2, 4, 6], [1, 3, 5, 7]]
    )
    total = finish_call(both).reshape(VARS, 8, 2, 2, 128).transpose(0, 1, 3, 2, 4)
    return total.reshape(VARS, 8, 2, 256)


def solution(mesh):
    in_specs = (
        P(None, "mem", "tile", None),
        P(None, None, "mem", "tile", None),
        P(),
        P(),
        P(),
        P(),
    )
    out_specs = P(None, "mem", "tile", None)
    return jax.shard_map(
        per_device, mesh=mesh, in_specs=in_specs, out_specs=out_specs, check_vma=False
    )
```

```python
import jax
import jax.numpy as jnp
from jax import lax
from jax.experimental import pallas as pl
from jax.experimental.pallas import tpu as pltpu
from jax.sharding import PartitionSpec as P

F32 = jnp.float32
BF16 = jnp.bfloat16
LEVELS = 64
VARS = 5
ROWS = 64
PITCH = 72
GROUP = 8
MEMBERS_AT_ONCE = 4
WIDE_GROUP = 4 * MEMBERS_AT_ONCE


def split(value):
    high = value.astype(BF16)
    low = (value - high.astype(F32)).astype(BF16)
    return high, low


def dot(a, b):
    return jnp.dot(a, b, preferred_element_type=F32)


def outer(matrix):
    return lax.dot_general(
        matrix, matrix, (((1,), (1,)), ((), ())), precision=lax.Precision.HIGHEST, preferred_element_type=F32
    )


def every_level(row):
    return pl.ds(row, LEVELS, stride=PITCH)


def level_rows(level):
    return pl.ds(pl.multiple_of(level * PITCH, 8), ROWS)


def spread(source, target):
    for level in range(LEVELS):
        target[level * PITCH : level * PITCH + ROWS, :] = source[level * ROWS : (level + 1) * ROWS, :]


def vertical_product(matrix, source, target):
    m_high, m_low = split(matrix)
    zero = jnp.zeros_like(m_high)
    left = jnp.concatenate(
        [jnp.concatenate([m_high, m_high], axis=1), jnp.concatenate([m_low, zero], axis=1)], axis=0
    )

    def half(step, carry):
        for pair in range(ROWS // 4):
            first = step * (ROWS // 2) + 2 * pair
            parts = [source[every_level(first + i), :] for i in range(2)]
            high, low = split(jnp.concatenate(parts, axis=1))
            result = dot(left, jnp.concatenate([high, low], axis=0))
            result = result[:LEVELS] + result[LEVELS:]
            for i in range(2):
                target[every_level(first + i), :] = result[:, 128 * i : 128 * (i + 1)]
        return carry

    lax.fori_loop(0, 2, half, 0)


def send_rows(result, out_ref, sem, step, count=GROUP):
    rows = pl.ds(pl.multiple_of(step * count, GROUP), count)
    view = result.reshape(LEVELS, PITCH, 128)
    return pltpu.make_async_copy(view.at[:, rows], out_ref.at[:, rows], sem.at[step])


def wait_rows(result, out_ref, sem, count=GROUP):
    for step in range(ROWS // count):
        send_rows(result, out_ref, sem, step, count).wait()


def smooth_along_x(scale_ref, smooth_x_ref, fields, covariances):
    matrix = smooth_x_ref[...]
    power = matrix
    for step in range(4):
        if step:
            power = jnp.dot(matrix, power, precision=lax.Precision.HIGHEST, preferred_element_type=F32)
        covariances[step] = outer(power)

    def level(q, carry):
        scale = scale_ref[q] - 1
        places = [[pl.ds(q * PITCH + 2 * half + r, ROWS // 4, stride=4) for half in range(2)] for r in range(2)]
        lines = [jnp.concatenate([fields[place, :] for place in pair], axis=1) for pair in places]
        product = jnp.dot(
            jnp.concatenate(lines, axis=0),
            covariances[scale],
            precision=lax.Precision.HIGHEST,
            preferred_element_type=F32,
        )
        for r in range(2):
            for half in range(2):
                fields[places[r][half], :] = product[
                    ROWS // 4 * r : ROWS // 4 * (r + 1), 128 * half : 128 * (half + 1)
                ]
        return carry

    lax.fori_loop(0, LEVELS, level, 0, unroll=4)


def adjoint_kernel(
    core_ref,
    scale_ref,
    dir_ref,
    perturb_ref,
    matrix_ref,
    smooth_x_ref,
    early_ref,
    out_ref,
    lines,
    controls,
    result,
    covariances,
    in_sem,
    out_sem,
):
    del early_ref
    pieces = []
    for c in range(8):
        part = pl.ds(8 * c, 8)
        pieces.append(pltpu.make_async_copy(perturb_ref.at[:, part], lines.at[:, part], in_sem.at[c]))
        pieces[c].start()

    def level(q, carry):
        total = None
        for v in range(VARS):
            direction = dir_ref[v, q]
            direction = jnp.concatenate([direction, direction], axis=0)
            term = lines[v, q].astype(F32).reshape(ROWS // 8, 8, 128) * direction[None]
            total = term if total is None else total + term
        controls[level_rows(q), :] = total.reshape(ROWS, 128)
        return carry

    for c in range(8):
        pieces[c].wait()
        lax.fori_loop(8 * c, 8 * c + 8, level, 0, unroll=2)
    vertical_product(matrix_ref[...].T, controls, result)

    @pl.when(core_ref[0] == 1)
    def _():
        smooth_along_x(scale_ref, smooth_x_ref, result, covariances)

    for step in range(ROWS // WIDE_GROUP):
        send_rows(result, out_ref, out_sem, step, WIDE_GROUP).start()
    wait_rows(result, out_ref, out_sem, WIDE_GROUP)


def chosen_covariance(scale, matrix):
    power = matrix
    chosen = matrix
    for step in range(2, 5):
        power = jnp.dot(matrix, power, precision=lax.Precision.HIGHEST, preferred_element_type=F32)
        chosen = jnp.where(scale == step, power, chosen)
    return split(outer(chosen))


def prepare_y_kernel(scale_ref, smooth_y_ref, y_ref):
    high, low = chosen_covariance(scale_ref[0], smooth_y_ref[...])
    y_ref[...] = jnp.concatenate([high, high, low], axis=1)


def prepare_kernel(scale_ref, smooth_y_ref, smooth_x_ref, y_ref, xh_ref, xl_ref):
    prepare_y_kernel(scale_ref, smooth_y_ref, y_ref)
    high, low = chosen_covariance(scale_ref[0], smooth_x_ref[...])
    xh_ref[...] = high
    xl_ref[...] = low


def smooth_kernel(core_ref, in_ref, y_ref, xh_ref, xl_ref, spent_ref, out_ref, source, result, out_sem):
    del spent_ref
    spread(in_ref, source)

    def run(with_x):
        y_both, y_low = y_ref[:, :256], y_ref[:, 256:]
        for step in range(ROWS // WIDE_GROUP):
            first = step * WIDE_GROUP
            halves = []
            for k in range(MEMBERS_AT_ONCE):
                for r in range(2):
                    parts = [source[every_level(first + 4 * k + 2 * half + r), :] for half in range(2)]
                    halves.append(jnp.concatenate(parts, axis=1))
            fields = jnp.concatenate(halves, axis=0)
            if with_x:
                high, low = split(fields)
                fields = dot(high, xh_ref[...]) + dot(low, xh_ref[...]) + dot(high, xl_ref[...])
            for k in range(MEMBERS_AT_ONCE):
                high, low = split(fields[128 * k : 128 * (k + 1)])
                smoothed = dot(y_both, jnp.concatenate([high, low], axis=0)) + dot(y_low, high)
                for r in range(2):
                    for half in range(2):
                        result[every_level(first + 4 * k + 2 * half + r), :] = smoothed[
                            64 * r : 64 * (r + 1), 128 * half : 128 * (half + 1)
                        ]
            send_rows(result, out_ref, out_sem, step, WIDE_GROUP).start()

    @pl.when(core_ref[0] == 0)
    def _():
        run(True)

    @pl.when(core_ref[0] == 1)
    def _():
        run(False)

    wait_rows(result, out_ref, out_sem, WIDE_GROUP)


def fetch_levels(parity, perturb_ref, lines, sem):
    pieces = []
    for chip in range(4):
        part = pl.ds(chip * 16 + parity * 8, 8)
        pieces.append(pltpu.make_async_copy(perturb_ref.at[:, part], lines.at[chip], sem.at[chip]))
        pieces[chip].start()
    return pieces


def increment_terms(parity, pieces, lines, forward_ref, out_ref):
    for chip in range(4):
        pieces[chip].wait()

        def level(i, carry, chip=chip):
            field = forward_ref[level_rows(chip * 16 + parity * 8 + i), :]
            for v in range(VARS):
                terms = lines[chip, v, i].astype(F32) * field
                eight = jnp.sum(terms.reshape(ROWS // 8, 8, 128), axis=0)
                out_ref[chip, v, i] = eight[:4] + eight[4:]
            return carry

        lax.fori_loop(0, 8, level, 0, unroll=2)


def give_kernel(core_ref, in_ref, perturb_ref, matrix_ref, forward_ref, give_ref, lines, source, sem):
    parity = 1 - core_ref[0]
    pieces = fetch_levels(parity, perturb_ref, lines, sem)
    spread(in_ref, source)
    vertical_product(matrix_ref[...], source, forward_ref)
    increment_terms(parity, pieces, lines, forward_ref, give_ref)


def keep_kernel(core_ref, forward_ref, perturb_ref, keep_ref, lines, sem):
    parity = core_ref[0]
    pieces = fetch_levels(parity, perturb_ref, lines, sem)
    increment_terms(parity, pieces, lines, forward_ref, keep_ref)


def finish_kernel(in_ref, out_ref):
    total = (in_ref[0] + in_ref[1]) + (in_ref[2] + in_ref[3])
    out_ref[...] = total / (128 - 1)


VMEM = pl.BlockSpec(memory_space=pltpu.VMEM)
SMEM = pl.BlockSpec(memory_space=pltpu.SMEM)
HBM = pl.BlockSpec(memory_space=pltpu.HBM)
FIELDS = jax.ShapeDtypeStruct((LEVELS, ROWS, 128), F32)
FLAT = jax.ShapeDtypeStruct((LEVELS * ROWS, 128), F32)
SHARE = jax.ShapeDtypeStruct((4, VARS, 8, 4, 128), F32)
SPREAD = jax.ShapeDtypeStruct((LEVELS * PITCH, 128), F32)
SPREAD_SCRATCH = pltpu.VMEM(SPREAD.shape, F32)
HALF_SCRATCH = pltpu.VMEM((4, VARS, 8, ROWS, 128), BF16)
X_SCRATCH = pltpu.VMEM((4, 256, 256), F32)
DMA = pltpu.SemaphoreType.DMA


def call(kernel, name, in_specs, out, flops, scratch=(), vmem=24, aliases=None):
    return pl.pallas_call(
        kernel,
        in_specs=in_specs,
        out_specs=[spec for spec, shape in out] if len(out) > 1 else out[0][0],
        out_shape=[shape for spec, shape in out] if len(out) > 1 else out[0][1],
        scratch_shapes=list(scratch),
        input_output_aliases=aliases or {},
        compiler_params=pltpu.CompilerParams(vmem_limit_bytes=vmem * 1024 * 1024),
        cost_estimate=pl.CostEstimate(flops=flops, bytes_accessed=4_000_000, transcendentals=0),
        name=name,
    )


adjoint_call = call(
    adjoint_kernel,
    "adjoint",
    [SMEM, SMEM, VMEM, HBM, VMEM, VMEM, HBM],
    [(HBM, FIELDS)],
    300_000_000,
    [pltpu.VMEM((VARS, LEVELS, ROWS, 128), BF16), SPREAD_SCRATCH, SPREAD_SCRATCH, X_SCRATCH, DMA((8,)), DMA((4,))],
    vmem=60,
)
COV_Y = jax.ShapeDtypeStruct((128, 384), BF16)
COV_X = jax.ShapeDtypeStruct((256, 256), BF16)
prepare_y_call = call(prepare_y_kernel, "prepare_y", [SMEM, VMEM], [(VMEM, COV_Y)], 300_000_000)
prepare_call = call(
    prepare_kernel,
    "prepare",
    [SMEM, VMEM, VMEM],
    [(VMEM, COV_Y), (VMEM, COV_X), (VMEM, COV_X)],
    1_000_000_000,
)
smooth_call = call(
    smooth_kernel,
    "smooth",
    [SMEM] + [VMEM] * 4 + [HBM],
    [(HBM, FIELDS)],
    1_200_000_000,
    [SPREAD_SCRATCH, SPREAD_SCRATCH, DMA((4,))],
    vmem=48,
    aliases={5: 0},
)
give_call = call(
    give_kernel,
    "give",
    [SMEM, VMEM, HBM, VMEM],
    [(VMEM, SPREAD), (VMEM, SHARE)],
    300_000_000,
    [HALF_SCRATCH, SPREAD_SCRATCH, DMA((4,))],
    vmem=48,
)
keep_call = call(
    keep_kernel,
    "keep",
    [SMEM, VMEM, HBM],
    [(VMEM, SHARE)],
    100_000_000,
    [HALF_SCRATCH, DMA((4,))],
    vmem=48,
)
finish_call = call(
    finish_kernel, "finish", [VMEM], [(VMEM, jax.ShapeDtypeStruct((VARS, 8, 4, 128), F32))], 1_000_000
)


def to_lines(array):
    lead = array.shape[:-2]
    n = len(lead)
    array = array.reshape(lead + (2, 2, 128))
    return array.transpose(tuple(range(n)) + (n + 1, n, n + 2)).reshape(lead + (4, 128))


def exchange(fields):
    return lax.all_to_all(fields, "tile", split_axis=0, concat_axis=0, tiled=True)


def flat(fields):
    return fields.reshape(FLAT.shape)


def per_device(search_dir, perturb, smooth_y, smooth_x, vertical, level_scale):
    core = lax.rem(lax.axis_index("mem"), 2)[None]
    lines = to_lines(perturb).reshape(VARS, LEVELS, ROWS, 128)
    full_dir = lax.all_gather(to_lines(search_dir), "mem", axis=1, tiled=True)

    def scale_and_y():
        scale = lax.dynamic_slice_in_dim(level_scale, lax.axis_index("tile"), 1)
        return scale, smooth_y.reshape(64, 2, 64, 2).transpose(1, 0, 3, 2).reshape(128, 128)

    second = core[0] == 1
    early = lax.cond(second, lambda: prepare_y_call(*scale_and_y()), lambda: jnp.zeros(COV_Y.shape, BF16))
    adjoint = adjoint_call(core, level_scale, full_dir, lines, vertical, smooth_x, early)
    cov_y, cov_xh, cov_xl = lax.cond(
        second,
        lambda: [early, jnp.zeros(COV_X.shape, BF16), jnp.zeros(COV_X.shape, BF16)],
        lambda: list(prepare_call(*scale_and_y(), smooth_x)),
    )

    smoothed = smooth_call(core, flat(exchange(adjoint)), cov_y, cov_xh, cov_xl, adjoint)
    forward, give = give_call(core, flat(exchange(smoothed)), lines, vertical)
    keep = keep_call(core, forward, lines)
    both = keep + lax.ppermute(give, "mem", [(m, m ^ 1) for m in range(8)])
    both = lax.all_to_all(
        both, "mem", split_axis=0, concat_axis=0, tiled=True, axis_index_groups=[[0, 2, 4, 6], [1, 3, 5, 7]]
    )
    total = finish_call(both).reshape(VARS, 8, 2, 2, 128).transpose(0, 1, 3, 2, 4)
    return total.reshape(VARS, 8, 2, 256)


def solution(mesh):
    in_specs = (
        P(None, "mem", "tile", None),
        P(None, None, "mem", "tile", None),
        P(),
        P(),
        P(),
        P(),
    )
    out_specs = P(None, "mem", "tile", None)
    return jax.shard_map(
        per_device, mesh=mesh, in_specs=in_specs, out_specs=out_specs, check_vma=False
    )
```

```python
import jax
import jax.numpy as jnp
from jax import lax
from jax.experimental import pallas as pl
from jax.experimental.pallas import tpu as pltpu
from jax.sharding import PartitionSpec as P

F32 = jnp.float32
BF16 = jnp.bfloat16
LEVELS = 64
VARS = 5
ROWS = 64
PITCH = 72
GROUP = 8
MEMBERS_AT_ONCE = 4
WIDE_GROUP = 4 * MEMBERS_AT_ONCE


def split(value):
    high = value.astype(BF16)
    low = (value - high.astype(F32)).astype(BF16)
    return high, low


def dot(a, b):
    return jnp.dot(a, b, preferred_element_type=F32)


def outer(matrix):
    return lax.dot_general(
        matrix, matrix, (((1,), (1,)), ((), ())), precision=lax.Precision.HIGHEST, preferred_element_type=F32
    )


def every_level(row):
    return pl.ds(row, LEVELS, stride=PITCH)


def level_rows(level):
    return pl.ds(pl.multiple_of(level * PITCH, 8), ROWS)


def spread(source, target):
    for level in range(LEVELS):
        target[level * PITCH : level * PITCH + ROWS, :] = source[level * ROWS : (level + 1) * ROWS, :]


def vertical_product(matrix, source, target):
    m_high, m_low = split(matrix)
    zero = jnp.zeros_like(m_high)
    left = jnp.concatenate(
        [jnp.concatenate([m_high, m_high], axis=1), jnp.concatenate([m_low, zero], axis=1)], axis=0
    )

    def half(step, carry):
        for pair in range(ROWS // 4):
            first = step * (ROWS // 2) + 2 * pair
            parts = [source[every_level(first + i), :] for i in range(2)]
            high, low = split(jnp.concatenate(parts, axis=1))
            result = dot(left, jnp.concatenate([high, low], axis=0))
            result = result[:LEVELS] + result[LEVELS:]
            for i in range(2):
                target[every_level(first + i), :] = result[:, 128 * i : 128 * (i + 1)]
        return carry

    lax.fori_loop(0, 2, half, 0)


def send_rows(result, out_ref, sem, step, count=GROUP):
    rows = pl.ds(pl.multiple_of(step * count, GROUP), count)
    view = result.reshape(LEVELS, PITCH, 128)
    return pltpu.make_async_copy(view.at[:, rows], out_ref.at[:, rows], sem.at[step])


def wait_rows(result, out_ref, sem, count=GROUP):
    for step in range(ROWS // count):
        send_rows(result, out_ref, sem, step, count).wait()


def smooth_along_x(scale_ref, smooth_x_ref, fields, covariances):
    matrix = smooth_x_ref[...]
    power = matrix
    for step in range(4):
        if step:
            power = jnp.dot(matrix, power, precision=lax.Precision.HIGHEST, preferred_element_type=F32)
        covariances[step] = outer(power)

    def level(q, carry):
        scale = scale_ref[q] - 1
        places = [[pl.ds(q * PITCH + 2 * half + r, ROWS // 4, stride=4) for half in range(2)] for r in range(2)]
        lines = [jnp.concatenate([fields[place, :] for place in pair], axis=1) for pair in places]
        product = jnp.dot(
            jnp.concatenate(lines, axis=0),
            covariances[scale],
            precision=lax.Precision.HIGHEST,
            preferred_element_type=F32,
        )
        for r in range(2):
            for half in range(2):
                fields[places[r][half], :] = product[
                    ROWS // 4 * r : ROWS // 4 * (r + 1), 128 * half : 128 * (half + 1)
                ]
        return carry

    lax.fori_loop(0, LEVELS, level, 0, unroll=4)


def adjoint_kernel(
    core_ref,
    scale_ref,
    dir_ref,
    perturb_ref,
    matrix_ref,
    smooth_x_ref,
    early_ref,
    out_ref,
    lines,
    controls,
    result,
    covariances,
    in_sem,
    out_sem,
):
    del early_ref
    pieces = []
    for c in range(8):
        part = pl.ds(8 * c, 8)
        pieces.append(pltpu.make_async_copy(perturb_ref.at[:, part], lines.at[:, part], in_sem.at[c]))
        pieces[c].start()

    def level(q, carry):
        total = None
        for v in range(VARS):
            direction = dir_ref[v, q]
            direction = jnp.concatenate([direction, direction], axis=0)
            term = lines[v, q].astype(F32).reshape(ROWS // 8, 8, 128) * direction[None]
            total = term if total is None else total + term
        controls[level_rows(q), :] = total.reshape(ROWS, 128)
        return carry

    for c in range(8):
        pieces[c].wait()
        lax.fori_loop(8 * c, 8 * c + 8, level, 0, unroll=2)
    matrix = matrix_ref[...].T

    @pl.when(core_ref[0] == 0)
    def _():
        vertical_product(matrix, controls, result)

    @pl.when(core_ref[0] == 1)
    def _():
        def pair(step, carry):
            parts = [controls[every_level(2 * step + i), :] for i in range(2)]
            product = jnp.dot(
                matrix,
                jnp.concatenate(parts, axis=1),
                precision=lax.Precision.HIGHEST,
                preferred_element_type=F32,
            )
            for i in range(2):
                result[every_level(2 * step + i), :] = product[:, 128 * i : 128 * (i + 1)]
            return carry

        lax.fori_loop(0, ROWS // 2, pair, 0, unroll=4)
        smooth_along_x(scale_ref, smooth_x_ref, result, covariances)

    for step in range(ROWS // WIDE_GROUP):
        send_rows(result, out_ref, out_sem, step, WIDE_GROUP).start()
    wait_rows(result, out_ref, out_sem, WIDE_GROUP)


def chosen_covariance(scale, matrix):
    power = matrix
    chosen = matrix
    for step in range(2, 5):
        power = jnp.dot(matrix, power, precision=lax.Precision.HIGHEST, preferred_element_type=F32)
        chosen = jnp.where(scale == step, power, chosen)
    return split(outer(chosen))


def prepare_y_kernel(scale_ref, smooth_y_ref, y_ref):
    high, low = chosen_covariance(scale_ref[0], smooth_y_ref[...])
    y_ref[...] = jnp.concatenate([high, high, low], axis=1)


def prepare_kernel(scale_ref, smooth_y_ref, smooth_x_ref, y_ref, xh_ref, xl_ref):
    prepare_y_kernel(scale_ref, smooth_y_ref, y_ref)
    high, low = chosen_covariance(scale_ref[0], smooth_x_ref[...])
    xh_ref[...] = high
    xl_ref[...] = low


def smooth_kernel(core_ref, in_ref, y_ref, xh_ref, xl_ref, spent_ref, out_ref, source, result, out_sem):
    del spent_ref
    spread(in_ref, source)

    def run(with_x):
        y_both, y_low = y_ref[:, :256], y_ref[:, 256:]
        for step in range(ROWS // WIDE_GROUP):
            first = step * WIDE_GROUP
            halves = []
            for k in range(MEMBERS_AT_ONCE):
                for r in range(2):
                    parts = [source[every_level(first + 4 * k + 2 * half + r), :] for half in range(2)]
                    halves.append(jnp.concatenate(parts, axis=1))
            fields = jnp.concatenate(halves, axis=0)
            if with_x:
                high, low = split(fields)
                fields = dot(high, xh_ref[...]) + dot(low, xh_ref[...]) + dot(high, xl_ref[...])
            for k in range(MEMBERS_AT_ONCE):
                high, low = split(fields[128 * k : 128 * (k + 1)])
                smoothed = dot(y_both, jnp.concatenate([high, low], axis=0)) + dot(y_low, high)
                for r in range(2):
                    for half in range(2):
                        result[every_level(first + 4 * k + 2 * half + r), :] = smoothed[
                            64 * r : 64 * (r + 1), 128 * half : 128 * (half + 1)
                        ]
            send_rows(result, out_ref, out_sem, step, WIDE_GROUP).start()

    @pl.when(core_ref[0] == 0)
    def _():
        run(True)

    @pl.when(core_ref[0] == 1)
    def _():
        run(False)

    wait_rows(result, out_ref, out_sem, WIDE_GROUP)


def fetch_levels(parity, perturb_ref, lines, sem):
    pieces = []
    for chip in range(4):
        part = pl.ds(chip * 16 + parity * 8, 8)
        pieces.append(pltpu.make_async_copy(perturb_ref.at[:, part], lines.at[chip], sem.at[chip]))
        pieces[chip].start()
    return pieces


def increment_terms(parity, pieces, lines, forward_ref, out_ref):
    for chip in range(4):
        pieces[chip].wait()

        def level(i, carry, chip=chip):
            field = forward_ref[level_rows(chip * 16 + parity * 8 + i), :]
            for v in range(VARS):
                terms = lines[chip, v, i].astype(F32) * field
                eight = jnp.sum(terms.reshape(ROWS // 8, 8, 128), axis=0)
                out_ref[chip, v, i] = eight[:4] + eight[4:]
            return carry

        lax.fori_loop(0, 8, level, 0, unroll=2)


def give_kernel(core_ref, in_ref, perturb_ref, matrix_ref, forward_ref, give_ref, lines, source, sem):
    parity = 1 - core_ref[0]
    pieces = fetch_levels(parity, perturb_ref, lines, sem)
    spread(in_ref, source)
    vertical_product(matrix_ref[...], source, forward_ref)
    increment_terms(parity, pieces, lines, forward_ref, give_ref)


def keep_kernel(core_ref, forward_ref, perturb_ref, keep_ref, lines, sem):
    parity = core_ref[0]
    pieces = fetch_levels(parity, perturb_ref, lines, sem)
    increment_terms(parity, pieces, lines, forward_ref, keep_ref)


def finish_kernel(in_ref, out_ref):
    total = (in_ref[0] + in_ref[1]) + (in_ref[2] + in_ref[3])
    out_ref[...] = total / (128 - 1)


VMEM = pl.BlockSpec(memory_space=pltpu.VMEM)
SMEM = pl.BlockSpec(memory_space=pltpu.SMEM)
HBM = pl.BlockSpec(memory_space=pltpu.HBM)
FIELDS = jax.ShapeDtypeStruct((LEVELS, ROWS, 128), F32)
FLAT = jax.ShapeDtypeStruct((LEVELS * ROWS, 128), F32)
SHARE = jax.ShapeDtypeStruct((4, VARS, 8, 4, 128), F32)
SPREAD = jax.ShapeDtypeStruct((LEVELS * PITCH, 128), F32)
SPREAD_SCRATCH = pltpu.VMEM(SPREAD.shape, F32)
HALF_SCRATCH = pltpu.VMEM((4, VARS, 8, ROWS, 128), BF16)
X_SCRATCH = pltpu.VMEM((4, 256, 256), F32)
DMA = pltpu.SemaphoreType.DMA


def call(kernel, name, in_specs, out, flops, scratch=(), vmem=24, aliases=None):
    return pl.pallas_call(
        kernel,
        in_specs=in_specs,
        out_specs=[spec for spec, shape in out] if len(out) > 1 else out[0][0],
        out_shape=[shape for spec, shape in out] if len(out) > 1 else out[0][1],
        scratch_shapes=list(scratch),
        input_output_aliases=aliases or {},
        compiler_params=pltpu.CompilerParams(vmem_limit_bytes=vmem * 1024 * 1024),
        cost_estimate=pl.CostEstimate(flops=flops, bytes_accessed=4_000_000, transcendentals=0),
        name=name,
    )


adjoint_call = call(
    adjoint_kernel,
    "adjoint",
    [SMEM, SMEM, VMEM, HBM, VMEM, VMEM, HBM],
    [(HBM, FIELDS)],
    300_000_000,
    [pltpu.VMEM((VARS, LEVELS, ROWS, 128), BF16), SPREAD_SCRATCH, SPREAD_SCRATCH, X_SCRATCH, DMA((8,)), DMA((4,))],
    vmem=60,
)
COV_Y = jax.ShapeDtypeStruct((128, 384), BF16)
COV_X = jax.ShapeDtypeStruct((256, 256), BF16)
prepare_y_call = call(prepare_y_kernel, "prepare_y", [SMEM, VMEM], [(VMEM, COV_Y)], 300_000_000)
prepare_call = call(
    prepare_kernel,
    "prepare",
    [SMEM, VMEM, VMEM],
    [(VMEM, COV_Y), (VMEM, COV_X), (VMEM, COV_X)],
    1_000_000_000,
)
smooth_call = call(
    smooth_kernel,
    "smooth",
    [SMEM] + [VMEM] * 4 + [HBM],
    [(HBM, FIELDS)],
    1_200_000_000,
    [SPREAD_SCRATCH, SPREAD_SCRATCH, DMA((4,))],
    vmem=48,
    aliases={5: 0},
)
give_call = call(
    give_kernel,
    "give",
    [SMEM, VMEM, HBM, VMEM],
    [(VMEM, SPREAD), (VMEM, SHARE)],
    300_000_000,
    [HALF_SCRATCH, SPREAD_SCRATCH, DMA((4,))],
    vmem=48,
)
keep_call = call(
    keep_kernel,
    "keep",
    [SMEM, VMEM, HBM],
    [(VMEM, SHARE)],
    100_000_000,
    [HALF_SCRATCH, DMA((4,))],
    vmem=48,
)
finish_call = call(
    finish_kernel, "finish", [VMEM], [(VMEM, jax.ShapeDtypeStruct((VARS, 8, 4, 128), F32))], 1_000_000
)


def to_lines(array):
    lead = array.shape[:-2]
    n = len(lead)
    array = array.reshape(lead + (2, 2, 128))
    return array.transpose(tuple(range(n)) + (n + 1, n, n + 2)).reshape(lead + (4, 128))


def exchange(fields):
    return lax.all_to_all(fields, "tile", split_axis=0, concat_axis=0, tiled=True)


def flat(fields):
    return fields.reshape(FLAT.shape)


def per_device(search_dir, perturb, smooth_y, smooth_x, vertical, level_scale):
    core = lax.rem(lax.axis_index("mem"), 2)[None]
    lines = to_lines(perturb).reshape(VARS, LEVELS, ROWS, 128)
    full_dir = lax.all_gather(to_lines(search_dir), "mem", axis=1, tiled=True)

    def scale_and_y():
        scale = lax.dynamic_slice_in_dim(level_scale, lax.axis_index("tile"), 1)
        return scale, smooth_y.reshape(64, 2, 64, 2).transpose(1, 0, 3, 2).reshape(128, 128)

    second = core[0] == 1
    early = lax.cond(second, lambda: prepare_y_call(*scale_and_y()), lambda: jnp.zeros(COV_Y.shape, BF16))
    adjoint = adjoint_call(core, level_scale, full_dir, lines, vertical, smooth_x, early)
    cov_y, cov_xh, cov_xl = lax.cond(
        second,
        lambda: [early, jnp.zeros(COV_X.shape, BF16), jnp.zeros(COV_X.shape, BF16)],
        lambda: list(prepare_call(*scale_and_y(), smooth_x)),
    )

    smoothed = smooth_call(core, flat(exchange(adjoint)), cov_y, cov_xh, cov_xl, adjoint)
    forward, give = give_call(core, flat(exchange(smoothed)), lines, vertical)
    keep = keep_call(core, forward, lines)
    both = keep + lax.ppermute(give, "mem", [(m, m ^ 1) for m in range(8)])
    both = lax.all_to_all(
        both, "mem", split_axis=0, concat_axis=0, tiled=True, axis_index_groups=[[0, 2, 4, 6], [1, 3, 5, 7]]
    )
    total = finish_call(both).reshape(VARS, 8, 2, 2, 128).transpose(0, 1, 3, 2, 4)
    return total.reshape(VARS, 8, 2, 256)


def solution(mesh):
    in_specs = (
        P(None, "mem", "tile", None),
        P(None, None, "mem", "tile", None),
        P(),
        P(),
        P(),
        P(),
    )
    out_specs = P(None, "mem", "tile", None)
    return jax.shard_map(
        per_device, mesh=mesh, in_specs=in_specs, out_specs=out_specs, check_vma=False
    )
```

```python
import jax
import jax.numpy as jnp
from jax import lax
from jax.experimental import pallas as pl
from jax.experimental.pallas import tpu as pltpu
from jax.sharding import PartitionSpec as P

F32 = jnp.float32
BF16 = jnp.bfloat16
LEVELS = 64
VARS = 5
ROWS = 64
PITCH = 72
GROUP = 8
MEMBERS_AT_ONCE = 4
WIDE_GROUP = 4 * MEMBERS_AT_ONCE


def split(value):
    high = value.astype(BF16)
    low = (value - high.astype(F32)).astype(BF16)
    return high, low


def dot(a, b):
    return jnp.dot(a, b, preferred_element_type=F32)


def outer(matrix):
    return lax.dot_general(
        matrix, matrix, (((1,), (1,)), ((), ())), precision=lax.Precision.HIGHEST, preferred_element_type=F32
    )


def every_level(row):
    return pl.ds(row, LEVELS, stride=PITCH)


def level_rows(level):
    return pl.ds(pl.multiple_of(level * PITCH, 8), ROWS)


def spread(source, target):
    for level in range(LEVELS):
        target[level * PITCH : level * PITCH + ROWS, :] = source[level * ROWS : (level + 1) * ROWS, :]


def vertical_product(matrix, source, target):
    m_high, m_low = split(matrix)
    zero = jnp.zeros_like(m_high)
    left = jnp.concatenate(
        [jnp.concatenate([m_high, m_high], axis=1), jnp.concatenate([m_low, zero], axis=1)], axis=0
    )

    def half(step, carry):
        for pair in range(ROWS // 4):
            first = step * (ROWS // 2) + 2 * pair
            parts = [source[every_level(first + i), :] for i in range(2)]
            high, low = split(jnp.concatenate(parts, axis=1))
            result = dot(left, jnp.concatenate([high, low], axis=0))
            result = result[:LEVELS] + result[LEVELS:]
            for i in range(2):
                target[every_level(first + i), :] = result[:, 128 * i : 128 * (i + 1)]
        return carry

    lax.fori_loop(0, 2, half, 0)


def send_rows(result, out_ref, sem, step, count=GROUP):
    rows = pl.ds(pl.multiple_of(step * count, GROUP), count)
    view = result.reshape(LEVELS, PITCH, 128)
    return pltpu.make_async_copy(view.at[:, rows], out_ref.at[:, rows], sem.at[step])


def wait_rows(result, out_ref, sem, count=GROUP):
    for step in range(ROWS // count):
        send_rows(result, out_ref, sem, step, count).wait()


def smooth_along_x(scale_ref, smooth_x_ref, fields, covariances):
    matrix = smooth_x_ref[...]
    power = matrix
    for step in range(4):
        if step:
            power = jnp.dot(matrix, power, precision=lax.Precision.HIGHEST, preferred_element_type=F32)
        covariances[step] = outer(power)

    def level(q, carry):
        scale = scale_ref[q] - 1
        places = [[pl.ds(q * PITCH + 2 * half + r, ROWS // 4, stride=4) for half in range(2)] for r in range(2)]
        lines = [jnp.concatenate([fields[place, :] for place in pair], axis=1) for pair in places]
        product = jnp.dot(
            jnp.concatenate(lines, axis=0),
            covariances[scale],
            precision=lax.Precision.HIGHEST,
            preferred_element_type=F32,
        )
        for r in range(2):
            for half in range(2):
                fields[places[r][half], :] = product[
                    ROWS // 4 * r : ROWS // 4 * (r + 1), 128 * half : 128 * (half + 1)
                ]
        return carry

    lax.fori_loop(0, LEVELS, level, 0, unroll=4)


def adjoint_kernel(
    core_ref,
    scale_ref,
    dir_ref,
    perturb_ref,
    matrix_ref,
    smooth_x_ref,
    early_ref,
    out_ref,
    lines,
    controls,
    result,
    covariances,
    in_sem,
    out_sem,
):
    del early_ref
    pieces = []
    for c in range(8):
        part = pl.ds(8 * c, 8)
        pieces.append(pltpu.make_async_copy(perturb_ref.at[:, part], lines.at[:, part], in_sem.at[c]))
        pieces[c].start()

    def level(q, carry):
        total = None
        for v in range(VARS):
            direction = dir_ref[v, q]
            direction = jnp.concatenate([direction, direction], axis=0)
            term = lines[v, q].astype(F32).reshape(ROWS // 8, 8, 128) * direction[None]
            total = term if total is None else total + term
        controls[level_rows(q), :] = total.reshape(ROWS, 128)
        return carry

    for c in range(8):
        pieces[c].wait()
        lax.fori_loop(8 * c, 8 * c + 8, level, 0, unroll=2)
    vertical_product(matrix_ref[...].T, controls, result)

    @pl.when(core_ref[0] == 1)
    def _():
        smooth_along_x(scale_ref, smooth_x_ref, result, covariances)

    for step in range(ROWS // WIDE_GROUP):
        send_rows(result, out_ref, out_sem, step, WIDE_GROUP).start()
    wait_rows(result, out_ref, out_sem, WIDE_GROUP)


def chosen_covariance(scale, matrix):
    power = matrix
    chosen = matrix
    for step in range(2, 5):
        power = jnp.dot(matrix, power, precision=lax.Precision.HIGHEST, preferred_element_type=F32)
        chosen = jnp.where(scale == step, power, chosen)
    return split(outer(chosen))


def prepare_y_kernel(scale_ref, smooth_y_ref, y_ref):
    high, low = chosen_covariance(scale_ref[0], smooth_y_ref[...])
    y_ref[...] = jnp.concatenate([high, high, low], axis=1)


def prepare_kernel(scale_ref, smooth_y_ref, smooth_x_ref, y_ref, xh_ref, xl_ref):
    prepare_y_kernel(scale_ref, smooth_y_ref, y_ref)
    high, low = chosen_covariance(scale_ref[0], smooth_x_ref[...])
    xh_ref[...] = high
    xl_ref[...] = low


def smooth_kernel(core_ref, in_ref, y_ref, xh_ref, xl_ref, spent_ref, out_ref, source, result, in_sem, out_sem):
    del spent_ref
    view = source.reshape(LEVELS, PITCH, 128)
    pieces = []
    for c in range(4):
        part = pl.ds(16 * c, 16)
        pieces.append(pltpu.make_async_copy(in_ref.at[part], view.at[part, pl.ds(0, ROWS)], in_sem.at[c]))
        pieces[c].start()
    for piece in pieces:
        piece.wait()

    def run(with_x):
        y_both, y_low = y_ref[:, :256], y_ref[:, 256:]
        for step in range(ROWS // WIDE_GROUP):
            first = step * WIDE_GROUP
            halves = []
            for k in range(MEMBERS_AT_ONCE):
                for r in range(2):
                    parts = [source[every_level(first + 4 * k + 2 * half + r), :] for half in range(2)]
                    halves.append(jnp.concatenate(parts, axis=1))
            fields = jnp.concatenate(halves, axis=0)
            if with_x:
                high, low = split(fields)
                fields = dot(high, xh_ref[...]) + dot(low, xh_ref[...]) + dot(high, xl_ref[...])
            for k in range(MEMBERS_AT_ONCE):
                high, low = split(fields[128 * k : 128 * (k + 1)])
                smoothed = dot(y_both, jnp.concatenate([high, low], axis=0)) + dot(y_low, high)
                for r in range(2):
                    for half in range(2):
                        result[every_level(first + 4 * k + 2 * half + r), :] = smoothed[
                            64 * r : 64 * (r + 1), 128 * half : 128 * (half + 1)
                        ]
            send_rows(result, out_ref, out_sem, step, WIDE_GROUP).start()

    @pl.when(core_ref[0] == 0)
    def _():
        run(True)

    @pl.when(core_ref[0] == 1)
    def _():
        run(False)

    wait_rows(result, out_ref, out_sem, WIDE_GROUP)


def fetch_levels(parity, perturb_ref, lines, sem):
    pieces = []
    for chip in range(4):
        part = pl.ds(chip * 16 + parity * 8, 8)
        pieces.append(pltpu.make_async_copy(perturb_ref.at[:, part], lines.at[chip], sem.at[chip]))
        pieces[chip].start()
    return pieces


def increment_terms(parity, pieces, lines, forward_ref, out_ref):
    for chip in range(4):
        pieces[chip].wait()

        def level(i, carry, chip=chip):
            field = forward_ref[level_rows(chip * 16 + parity * 8 + i), :]
            for v in range(VARS):
                terms = lines[chip, v, i].astype(F32) * field
                eight = jnp.sum(terms.reshape(ROWS // 8, 8, 128), axis=0)
                out_ref[chip, v, i] = eight[:4] + eight[4:]
            return carry

        lax.fori_loop(0, 8, level, 0, unroll=2)


def give_kernel(core_ref, in_ref, perturb_ref, matrix_ref, forward_ref, give_ref, lines, source, sem):
    parity = 1 - core_ref[0]
    pieces = fetch_levels(parity, perturb_ref, lines, sem)
    spread(in_ref, source)
    vertical_product(matrix_ref[...], source, forward_ref)
    increment_terms(parity, pieces, lines, forward_ref, give_ref)


def keep_kernel(core_ref, forward_ref, perturb_ref, keep_ref, lines, sem):
    parity = core_ref[0]
    pieces = fetch_levels(parity, perturb_ref, lines, sem)
    increment_terms(parity, pieces, lines, forward_ref, keep_ref)


def finish_kernel(in_ref, out_ref):
    total = (in_ref[0] + in_ref[1]) + (in_ref[2] + in_ref[3])
    out_ref[...] = total / (128 - 1)


VMEM = pl.BlockSpec(memory_space=pltpu.VMEM)
SMEM = pl.BlockSpec(memory_space=pltpu.SMEM)
HBM = pl.BlockSpec(memory_space=pltpu.HBM)
FIELDS = jax.ShapeDtypeStruct((LEVELS, ROWS, 128), F32)
FLAT = jax.ShapeDtypeStruct((LEVELS * ROWS, 128), F32)
SHARE = jax.ShapeDtypeStruct((4, VARS, 8, 4, 128), F32)
SPREAD = jax.ShapeDtypeStruct((LEVELS * PITCH, 128), F32)
SPREAD_SCRATCH = pltpu.VMEM(SPREAD.shape, F32)
HALF_SCRATCH = pltpu.VMEM((4, VARS, 8, ROWS, 128), BF16)
X_SCRATCH = pltpu.VMEM((4, 256, 256), F32)
DMA = pltpu.SemaphoreType.DMA


def call(kernel, name, in_specs, out, flops, scratch=(), vmem=24, aliases=None):
    return pl.pallas_call(
        kernel,
        in_specs=in_specs,
        out_specs=[spec for spec, shape in out] if len(out) > 1 else out[0][0],
        out_shape=[shape for spec, shape in out] if len(out) > 1 else out[0][1],
        scratch_shapes=list(scratch),
        input_output_aliases=aliases or {},
        compiler_params=pltpu.CompilerParams(vmem_limit_bytes=vmem * 1024 * 1024),
        cost_estimate=pl.CostEstimate(flops=flops, bytes_accessed=4_000_000, transcendentals=0),
        name=name,
    )


adjoint_call = call(
    adjoint_kernel,
    "adjoint",
    [SMEM, SMEM, VMEM, HBM, VMEM, VMEM, HBM],
    [(HBM, FIELDS)],
    300_000_000,
    [pltpu.VMEM((VARS, LEVELS, ROWS, 128), BF16), SPREAD_SCRATCH, SPREAD_SCRATCH, X_SCRATCH, DMA((8,)), DMA((4,))],
    vmem=60,
)
COV_Y = jax.ShapeDtypeStruct((128, 384), BF16)
COV_X = jax.ShapeDtypeStruct((256, 256), BF16)
prepare_y_call = call(prepare_y_kernel, "prepare_y", [SMEM, VMEM], [(VMEM, COV_Y)], 300_000_000)
prepare_call = call(
    prepare_kernel,
    "prepare",
    [SMEM, VMEM, VMEM],
    [(VMEM, COV_Y), (VMEM, COV_X), (VMEM, COV_X)],
    1_000_000_000,
)
smooth_call = call(
    smooth_kernel,
    "smooth",
    [SMEM, HBM] + [VMEM] * 3 + [HBM],
    [(HBM, FIELDS)],
    1_200_000_000,
    [SPREAD_SCRATCH, SPREAD_SCRATCH, DMA((4,)), DMA((4,))],
    vmem=48,
    aliases={5: 0},
)
give_call = call(
    give_kernel,
    "give",
    [SMEM, VMEM, HBM, VMEM],
    [(VMEM, SPREAD), (VMEM, SHARE)],
    300_000_000,
    [HALF_SCRATCH, SPREAD_SCRATCH, DMA((4,))],
    vmem=48,
)
keep_call = call(
    keep_kernel,
    "keep",
    [SMEM, VMEM, HBM],
    [(VMEM, SHARE)],
    100_000_000,
    [HALF_SCRATCH, DMA((4,))],
    vmem=48,
)
finish_call = call(
    finish_kernel, "finish", [VMEM], [(VMEM, jax.ShapeDtypeStruct((VARS, 8, 4, 128), F32))], 1_000_000
)


def to_lines(array):
    lead = array.shape[:-2]
    n = len(lead)
    array = array.reshape(lead + (2, 2, 128))
    return array.transpose(tuple(range(n)) + (n + 1, n, n + 2)).reshape(lead + (4, 128))


def exchange(fields):
    return lax.all_to_all(fields, "tile", split_axis=0, concat_axis=0, tiled=True)


def flat(fields):
    return fields.reshape(FLAT.shape)


def per_device(search_dir, perturb, smooth_y, smooth_x, vertical, level_scale):
    core = lax.rem(lax.axis_index("mem"), 2)[None]
    lines = to_lines(perturb).reshape(VARS, LEVELS, ROWS, 128)
    full_dir = lax.all_gather(to_lines(search_dir), "mem", axis=1, tiled=True)

    def scale_and_y():
        scale = lax.dynamic_slice_in_dim(level_scale, lax.axis_index("tile"), 1)
        return scale, smooth_y.reshape(64, 2, 64, 2).transpose(1, 0, 3, 2).reshape(128, 128)

    second = core[0] == 1
    early = lax.cond(second, lambda: prepare_y_call(*scale_and_y()), lambda: jnp.zeros(COV_Y.shape, BF16))
    adjoint = adjoint_call(core, level_scale, full_dir, lines, vertical, smooth_x, early)
    cov_y, cov_xh, cov_xl = lax.cond(
        second,
        lambda: [early, jnp.zeros(COV_X.shape, BF16), jnp.zeros(COV_X.shape, BF16)],
        lambda: list(prepare_call(*scale_and_y(), smooth_x)),
    )

    smoothed = smooth_call(core, exchange(adjoint), cov_y, cov_xh, cov_xl, adjoint)
    forward, give = give_call(core, flat(exchange(smoothed)), lines, vertical)
    keep = keep_call(core, forward, lines)
    both = keep + lax.ppermute(give, "mem", [(m, m ^ 1) for m in range(8)])
    both = lax.all_to_all(
        both, "mem", split_axis=0, concat_axis=0, tiled=True, axis_index_groups=[[0, 2, 4, 6], [1, 3, 5, 7]]
    )
    total = finish_call(both).reshape(VARS, 8, 2, 2, 128).transpose(0, 1, 3, 2, 4)
    return total.reshape(VARS, 8, 2, 256)


def solution(mesh):
    in_specs = (
        P(None, "mem", "tile", None),
        P(None, None, "mem", "tile", None),
        P(),
        P(),
        P(),
        P(),
    )
    out_specs = P(None, "mem", "tile", None)
    return jax.shard_map(
        per_device, mesh=mesh, in_specs=in_specs, out_specs=out_specs, check_vma=False
    )
```
